256 devices in a mesh: row: 16 (over z_hi, y, core), col: 16 (over z_lo, x).
Axes of the slice: x: 4, y: 4, z: 8 (z_hi: 2, z_lo: 4; z = z_hi * 4 + z_lo), core: 2. Of those that a mesh axis runs over, the one named last changes fastest.
Arguments:
- tensor: float32 [32, 4096, 4096], P(None, 'row', 'col'), may hold values from -120 to 120
- factor_b: float32 [4096, 256], P('col', 'row'), may hold values from -1 to 1
- factor_c: float32 [32, 256], replicated, may hold values from -5 to 5
Outputs:
- factor_a: float32 [4096, 256], P(('row', 'col'))
- col_scale: float32 [256], replicated
The draws below stay inside these ranges and needn't reach their ends.
All inputs are finite; a program needn't handle non-finite values.
Results may differ from the reference program's by a relative error of at most 0.0003.
Values sent between devices are 32-bit elements; how exact they have to be, the bound alone decides.
No kernel may reach another device: no remote copies, remote signals or barrier semaphores. Data moves between devices by JAX's collectives and lax.ppermute only.
A program may use at most 64 MiB of HBM per device.

```python
import jax
import jax.numpy as jnp
from jax import lax

K = 32
R = 256
I = 4096
J = 4096


def draw_tensor(key, part):
    key = jax.random.fold_in(key, 11)
    first, second = jax.random.split(key, 2)
    rise = 3.0 ** (jnp.arange(I, dtype=jnp.float32) / I)
    spread = jnp.exp(jax.random.uniform(second, (I,), minval=0.0, maxval=jnp.log(3.4)))
    values = jnp.clip(jax.random.normal(first, (K, I, J)), -6.0, 6.0)
    return (values * (rise * spread)[None, :, None]).astype(jnp.float32)


def draw_factor_b(key, part):
    key = jax.random.fold_in(key, 12)
    first, second = jax.random.split(key)
    own = jnp.clip(jax.random.normal(first, (J, R)), -4.0, 4.0)
    shared = jnp.clip(jax.random.normal(second, (J, 1)), -4.0, 4.0)
    return ((own + shared) / jnp.sqrt(J * 1.0)).astype(jnp.float32)


def draw_factor_c(key, part):
    key = jax.random.fold_in(key, 13)
    first, second, third = jax.random.split(key, 3)
    columns = jnp.exp(jax.random.uniform(third, (R,), minval=0.0, maxval=jnp.log(3.0)))
    own = jnp.clip(jax.random.normal(first, (K, R)), -4.0, 4.0)
    shared = jnp.clip(jax.random.normal(second, (K, 1)), -4.0, 4.0)
    return ((own + shared) * columns[None, :] / jnp.sqrt(K * 1.0)).astype(jnp.float32)


def setup_inputs(seed: int = 0) -> dict:
    arg_keys = jax.random.split(jax.random.key(seed), 4)
    tensor = draw_tensor(jax.random.fold_in(arg_keys[3], 71), 0)
    factor_b = draw_factor_b(jax.random.fold_in(arg_keys[3], 71), 0)
    factor_c = draw_factor_c(jax.random.fold_in(arg_keys[3], 71), 0)
    return {"tensor": tensor, "factor_b": factor_b, "factor_c": factor_c}


eps = 1e-06

def reference(tensor, factor_b, factor_c):
    high = lax.Precision.HIGHEST
    gram = jnp.dot(factor_b.T.astype(jnp.float32), factor_b.astype(jnp.float32), precision=high, preferred_element_type=jnp.float32) * jnp.dot(factor_c.T.astype(jnp.float32), factor_c.astype(jnp.float32), precision=high, preferred_element_type=jnp.float32)
    depth, rows_i, cols_j = tensor.shape
    ranks = factor_b.shape[1]

    def frame_step(total, pair):
        slab, weight = pair
        product = jnp.dot(slab.astype(jnp.float32), factor_b.astype(jnp.float32), precision=high, preferred_element_type=jnp.float32)
        return (total + product * weight[None, :], None)
    start = jnp.zeros((rows_i, ranks), jnp.float32)
    mttkrp, unused = lax.scan(frame_step, start, (tensor, factor_c))
    lower = jnp.linalg.cholesky(gram)
    half = lax.linalg.triangular_solve(lower, mttkrp, left_side=False, lower=True, transpose_a=True)
    solved = lax.linalg.triangular_solve(lower, half, left_side=False, lower=True, transpose_a=False)
    col_scale = jnp.sqrt(lax.optimization_barrier(jnp.sum(solved * solved, axis=0)) / rows_i + eps)
    return (solved / col_scale, col_scale)
```

```python
import jax
import jax.numpy as jnp
from jax import lax
from jax.sharding import PartitionSpec as P

eps = 1e-06


def gather_blocks(block, axis):
    count = lax.axis_size(axis)
    copies = jnp.broadcast_to(block[None], (count,) + block.shape)
    return lax.all_to_all(copies, axis, 0, 0)


def scatter_sum(whole, axis):
    count = lax.axis_size(axis)
    pieces = whole.reshape(count, whole.shape[0] // count, whole.shape[1])
    return jnp.sum(lax.all_to_all(pieces, axis, 0, 0), axis=0)


def contract_rows(slab, block_bt, factor_c):
    depth, count, cols_j = slab.shape
    product = lax.dot_general(
        slab.reshape(depth * count, cols_j),
        block_bt,
        (((1,), (1,)), ((), ())),
        precision=lax.Precision.HIGH,
        preferred_element_type=jnp.float32,
    )
    product = product.reshape(depth, count, block_bt.shape[0])
    return jnp.sum(product * factor_c[:, None, :], axis=0)


def local(tensor, factor_b, factor_c):
    high = lax.Precision.HIGHEST
    depth, rows_i, cols_j = tensor.shape
    ranks = factor_c.shape[1]
    block_bt = gather_blocks(factor_b.T, "row").reshape(ranks, cols_j)
    partial_gram = lax.dot_general(
        block_bt, block_bt, (((1,), (1,)), ((), ())), precision=high,
        preferred_element_type=jnp.float32,
    )
    gram_c = jnp.dot(factor_c.T, factor_c, precision=high, preferred_element_type=jnp.float32)
    gram_rows = scatter_sum(partial_gram, "col")
    gram_b = gather_blocks(gram_rows, "col").reshape(ranks, ranks)
    mine = scatter_sum(contract_rows(tensor, block_bt, factor_c), "col")
    gram = gram_b * gram_c
    lower = jnp.linalg.cholesky(gram)
    half = lax.linalg.triangular_solve(lower, mine, left_side=False, lower=True, transpose_a=True)
    solved = lax.linalg.triangular_solve(
        lower, half, left_side=False, lower=True, transpose_a=False
    )
    squares = gather_blocks(jnp.sum(solved * solved, axis=0)[None], ("row", "col"))
    squares = jnp.sum(squares[:, 0], axis=0)
    col_scale = jnp.sqrt(squares / (rows_i * lax.axis_size("row")) + eps)
    return (solved / col_scale, col_scale)


def solution(mesh):
    return jax.shard_map(
        local,
        mesh=mesh,
        in_specs=(P(None, "row", "col"), P("col", "row"), P()),
        out_specs=(P(("row", "col"), None), P()),
        check_vma=False,
    )
```

```python
import functools

import jax
import jax.numpy as jnp
from jax import lax
from jax.experimental import pallas as pl
from jax.experimental.pallas import tpu as pltpu
from jax.sharding import PartitionSpec as P

eps = 1e-06
high = lax.Precision.HIGHEST
f32 = jnp.float32
bf16 = jnp.bfloat16
limit = 16 * 1024 * 1024
pivots = 16
lanes = 128
frames = 4
both = ("row", "col")
nt = (((1,), (1,)), ((), ()))


def interleave(core, mine, other):
    first = core == 0
    return jnp.concatenate(
        [jnp.where(first, mine, other), jnp.where(first, other, mine)], axis=1
    )


def gram_kernel(core_ref, mine_ref, other_ref, block_ref, part_ref):
    mine = mine_ref[...]
    count, width, cols_j = mine.shape
    block = interleave(core_ref[0], mine, other_ref[...]).reshape(2 * count * width, cols_j)
    block_ref[...] = block
    part = lax.dot_general(
        mine.reshape(count * width, cols_j), block, nt, precision=high, preferred_element_type=f32
    )
    part_ref[...] = part.reshape(part_ref.shape)


def partial_gram(core, mine, other, peers):
    count, width, cols_j = mine.shape
    ranks = 2 * count * width
    return pl.pallas_call(
        gram_kernel,
        out_shape=(
            jax.ShapeDtypeStruct((ranks, cols_j), f32),
            jax.ShapeDtypeStruct((peers, ranks // 2 // peers, ranks), f32),
        ),
        in_specs=[pl.BlockSpec(memory_space=pltpu.SMEM)]
        + [pl.BlockSpec(memory_space=pltpu.VMEM)] * 2,
        out_specs=[pl.BlockSpec(memory_space=pltpu.VMEM)] * 2,
        compiler_params=pltpu.CompilerParams(vmem_limit_bytes=limit),
        name="gram_part",
    )(core, mine, other)


def halves(value):
    top = value.astype(bf16)
    return top, (value - top.astype(f32)).astype(bf16)


def mttkrp_kernel(slab_ref, block_ref, c_ref, out_ref, split_ref):
    step = pl.program_id(0)

    @pl.when(step == 0)
    def _():
        top, low = halves(block_ref[...])
        split_ref[...] = jnp.concatenate([top, low, top], axis=1)
        out_ref[...] = jnp.zeros_like(out_ref)

    weights = split_ref[...]
    total = out_ref[...]
    for k in range(slab_ref.shape[0]):
        top, low = halves(slab_ref[k])
        product = lax.dot_general(
            jnp.concatenate([top, top, low], axis=1), weights, nt, preferred_element_type=f32
        )
        total += product * c_ref[k : k + 1]
    out_ref[...] = total


def mttkrp(slab, block, factor_c):
    depth, rows_i, cols_j = slab.shape
    ranks = block.shape[0]
    return pl.pallas_call(
        mttkrp_kernel,
        grid=(depth // frames,),
        out_shape=jax.ShapeDtypeStruct((rows_i, ranks), f32),
        in_specs=[
            pl.BlockSpec((frames, rows_i, cols_j), lambda s: (s, 0, 0)),
            pl.BlockSpec((ranks, cols_j), lambda s: (0, 0)),
            pl.BlockSpec((None, frames, ranks), lambda s: (s, 0, 0)),
        ],
        out_specs=pl.BlockSpec((rows_i, ranks), lambda s: (0, 0)),
        scratch_shapes=[pltpu.VMEM((ranks, 3 * cols_j), bf16)],
        compiler_params=pltpu.CompilerParams(vmem_limit_bytes=limit),
        cost_estimate=pl.CostEstimate(
            flops=6 * depth * rows_i * cols_j * ranks,
            bytes_accessed=4 * depth * rows_i * cols_j,
            transcendentals=0,
        ),
        name="mttkrp",
    )(slab, block, factor_c.reshape(depth // frames, frames, ranks))


def pack_kernel(parts_ref, terms_ref, out_ref):
    rows = parts_ref.shape[1]
    total = jnp.sum(parts_ref[...], axis=0)
    out_ref[:, :rows] = jnp.broadcast_to(total[None], parts_ref.shape)
    out_ref[:, rows:] = terms_ref[...].reshape(out_ref[:, rows:].shape)


def pack(parts, terms):
    peers, rows, ranks = parts.shape
    return pl.pallas_call(
        pack_kernel,
        out_shape=jax.ShapeDtypeStruct((peers, rows + terms.shape[0] // peers, ranks), f32),
        compiler_params=pltpu.CompilerParams(vmem_limit_bytes=limit),
        name="pack",
    )(parts, terms)


def invert(gram_ref):
    size = gram_ref.shape[0]

    def step(_, carry):
        head = gram_ref[:pivots]
        row = lax.broadcasted_iota(jnp.int32, (pivots, lanes), 0)
        lane = lax.broadcasted_iota(jnp.int32, (pivots, lanes), 1)
        cols = [jnp.broadcast_to(head[:, q : q + 1], (pivots, lanes)) for q in range(pivots)]
        turned = pltpu.roll(head, size - pivots, axis=1)
        left, right = turned[:, :lanes], turned[:, lanes:]
        for q in range(pivots):
            here = row == q
            col = cols[q]
            inverse = jnp.broadcast_to(1.0 / col[q : q + 1], col.shape)
            factor = jnp.where(here, -inverse, col * inverse)
            for p in range(q + 1, pivots):
                top = jnp.broadcast_to(cols[p][q : q + 1], col.shape)
                cols[p] = jnp.where(here, 0.0, cols[p]) - factor * top
            own = lane == lanes - pivots + q
            top = jnp.broadcast_to(left[q : q + 1], left.shape)
            left = jnp.where(here, 0.0, left) - factor * top
            top = jnp.where(own, 1.0, jnp.broadcast_to(right[q : q + 1], right.shape))
            right = jnp.where(here | own, 0.0, right) - factor * top
        done = jnp.concatenate([left, right], axis=1)
        rest = gram_ref[pivots:]
        lane = lax.broadcasted_iota(jnp.int32, rest.shape, 1)
        base = pltpu.roll(jnp.where(lane < pivots, 0.0, rest), size - pivots, axis=1)
        update = jnp.dot(rest[:, :pivots], done, precision=high, preferred_element_type=f32)
        gram_ref[: size - pivots] = base - update
        gram_ref[size - pivots :] = done
        return carry

    lax.fori_loop(0, size // pivots, step, 0)


def solve_kernel(core_ref, packed_ref, other_ref, c_ref, solved_ref, squares_ref, gram_ref):
    other = other_ref[...]
    peers, rows, ranks = other.shape
    shape = (peers // 2, 2 * rows, ranks)
    gram_b = interleave(
        core_ref[0], packed_ref[:, :rows].reshape(shape), other.reshape(shape)
    ).reshape(ranks, ranks)
    c = c_ref[...]
    gram_c = lax.dot_general(
        c, c, (((0,), (0,)), ((), ())), precision=high, preferred_element_type=f32
    )
    gram_ref[...] = gram_b * gram_c
    invert(gram_ref)
    mine = jnp.sum(packed_ref[:, rows:], axis=0)
    solved = jnp.dot(mine, gram_ref[...], precision=high, preferred_element_type=f32)
    solved_ref[...] = solved
    squares_ref[...] = jnp.sum(solved * solved, axis=0, keepdims=True)


def solve(core, packed, other, factor_c):
    peers, rows, ranks = other.shape
    return pl.pallas_call(
        solve_kernel,
        out_shape=(
            jax.ShapeDtypeStruct((packed.shape[1] - rows, ranks), f32),
            jax.ShapeDtypeStruct((1, ranks), f32),
        ),
        in_specs=[pl.BlockSpec(memory_space=pltpu.SMEM)]
        + [pl.BlockSpec(memory_space=pltpu.VMEM)] * 3,
        scratch_shapes=[pltpu.VMEM((ranks, ranks), f32)],
        compiler_params=pltpu.CompilerParams(vmem_limit_bytes=limit),
        name="solve",
    )(core, packed, other, factor_c)


def local(tensor, factor_b, factor_c):
    depth, rows_i, cols_j = tensor.shape
    n_row, n_col = lax.axis_size("row"), lax.axis_size("col")
    core = (lax.axis_index("row") % 2).astype(jnp.int32)[None]
    chips = n_row // 2
    same_core = [[2 * chip + core for chip in range(chips)] for core in range(2)]
    swap = [(i, i ^ 1) for i in range(n_row)]
    width = factor_b.shape[1]

    copies = jnp.broadcast_to(factor_b.T[None], (chips, width, cols_j))
    mine = lax.all_to_all(copies, "row", 0, 0, axis_index_groups=same_core)
    other = lax.ppermute(mine, "row", swap)
    block, parts = partial_gram(core, mine, other, n_col)
    parts = lax.all_to_all(parts, "col", 0, 0)
    terms = mttkrp(tensor, block, factor_c)
    packed = lax.all_to_all(pack(parts, terms), "col", 0, 0)
    other = lax.ppermute(packed[:, : parts.shape[1]], "row", swap)
    solved, squares = solve(core, packed, other, factor_c)
    squares = squares + lax.ppermute(squares, "row", swap)
    same_core = [
        [(2 * chip + core) * n_col + c for chip in range(chips) for c in range(n_col)]
        for core in range(2)
    ]
    copies = jnp.broadcast_to(squares[None], (chips * n_col,) + squares.shape)
    squares = lax.all_to_all(copies, both, 0, 0, axis_index_groups=same_core)
    squares = jnp.sum(squares[:, 0], axis=0)
    col_scale = jnp.sqrt(squares / (rows_i * n_row) + eps)
    return (solved / col_scale, col_scale)


def solution(mesh):
    return jax.shard_map(
        local,
        mesh=mesh,
        in_specs=(P(None, "row", "col"), P("col", "row"), P()),
        out_specs=(P(both, None), P()),
        check_vma=False,
    )
```

```python
import functools

import jax
import jax.numpy as jnp
from jax import lax
from jax.experimental import pallas as pl
from jax.experimental.pallas import tpu as pltpu
from jax.sharding import PartitionSpec as P

eps = 1e-06
high = lax.Precision.HIGHEST
f32 = jnp.float32
bf16 = jnp.bfloat16
limit = 16 * 1024 * 1024
wide = 52 * 1024 * 1024
pivots = 16
lanes = 128
frames = (4, 12, 16)
both = ("row", "col")
nt = (((1,), (1,)), ((), ()))


def interleave(core, mine, other):
    first = core == 0
    return jnp.concatenate(
        [jnp.where(first, mine, other), jnp.where(first, other, mine)], axis=1
    )


def gram_kernel(core_ref, mine_ref, other_ref, block_ref, part_ref):
    mine = mine_ref[...]
    count, width, cols_j = mine.shape
    block = interleave(core_ref[0], mine, other_ref[...]).reshape(2 * count * width, cols_j)
    block_ref[...] = block
    part = lax.dot_general(
        mine.reshape(count * width, cols_j), block, nt, precision=high, preferred_element_type=f32
    )
    part_ref[...] = part.reshape(part_ref.shape)


def partial_gram(core, mine, other, peers):
    count, width, cols_j = mine.shape
    ranks = 2 * count * width
    return pl.pallas_call(
        gram_kernel,
        out_shape=(
            jax.ShapeDtypeStruct((ranks, cols_j), f32),
            jax.ShapeDtypeStruct((peers, ranks // 2 // peers, ranks), f32),
        ),
        in_specs=[pl.BlockSpec(memory_space=pltpu.SMEM)]
        + [pl.BlockSpec(memory_space=pltpu.VMEM)] * 2,
        out_specs=[pl.BlockSpec(memory_space=pltpu.VMEM)] * 2,
        compiler_params=pltpu.CompilerParams(vmem_limit_bytes=limit),
        name="gram_part",
    )(core, mine, other)


def halves(value):
    top = value.astype(bf16)
    return top, (value - top.astype(f32)).astype(bf16)


def mttkrp_kernel(slab_hbm, block_ref, c_hbm, out_ref, gram_c_ref, slab_ref, c_ref, arrived):
    pieces = []
    first = 0
    for part, count in enumerate(frames):
        here = pl.ds(first, count)
        copy = pltpu.make_async_copy(slab_hbm.at[here], slab_ref.at[here], arrived.at[part])
        pieces.append((copy, range(first, first + count)))
        first += count
    c_copy = pltpu.make_async_copy(c_hbm, c_ref, arrived.at[len(frames)])
    c_copy.start()
    for copy, _ in pieces:
        copy.start()
    c_copy.wait()
    c = c_ref[...]
    gram_c_ref[...] = lax.dot_general(
        c, c, (((0,), (0,)), ((), ())), precision=high, preferred_element_type=f32
    )
    top, low = halves(block_ref[...])
    weights = jnp.concatenate([top, low, top], axis=1)
    total = jnp.zeros(out_ref.shape, f32)
    for copy, here in pieces:
        copy.wait()
        for k in here:
            top, low = halves(slab_ref[k])
            product = lax.dot_general(
                jnp.concatenate([top, top, low], axis=1), weights, nt, preferred_element_type=f32
            )
            total += product * c[k : k + 1]
    out_ref[...] = total


def mttkrp(slab, block, factor_c):
    depth, rows_i, cols_j = slab.shape
    ranks = block.shape[0]
    return pl.pallas_call(
        mttkrp_kernel,
        out_shape=(
            jax.ShapeDtypeStruct((rows_i, ranks), f32),
            jax.ShapeDtypeStruct((ranks, ranks), f32),
        ),
        in_specs=[
            pl.BlockSpec(memory_space=pl.ANY),
            pl.BlockSpec(memory_space=pltpu.VMEM),
            pl.BlockSpec(memory_space=pl.ANY),
        ],
        scratch_shapes=[
            pltpu.VMEM(slab.shape, f32),
            pltpu.VMEM(factor_c.shape, f32),
            pltpu.SemaphoreType.DMA((len(frames) + 1,)),
        ],
        compiler_params=pltpu.CompilerParams(vmem_limit_bytes=wide),
        cost_estimate=pl.CostEstimate(
            flops=6 * depth * rows_i * cols_j * ranks,
            bytes_accessed=4 * depth * rows_i * cols_j,
            transcendentals=0,
        ),
        name="mttkrp",
    )(slab, block, factor_c)


def pack_kernel(parts_ref, terms_ref, out_ref):
    rows = parts_ref.shape[1]
    total = jnp.sum(parts_ref[...], axis=0)
    out_ref[:, :rows] = jnp.broadcast_to(total[None], parts_ref.shape)
    out_ref[:, rows:] = terms_ref[...].reshape(out_ref[:, rows:].shape)


def pack(parts, terms):
    peers, rows, ranks = parts.shape
    return pl.pallas_call(
        pack_kernel,
        out_shape=jax.ShapeDtypeStruct((peers, rows + terms.shape[0] // peers, ranks), f32),
        compiler_params=pltpu.CompilerParams(vmem_limit_bytes=limit),
        name="pack",
    )(parts, terms)


def split(value):
    top = value.astype(bf16)
    rest = value - top.astype(f32)
    middle = rest.astype(bf16)
    return top, middle, (rest - middle.astype(f32)).astype(bf16)


def left_parts(value):
    top, middle, low = split(value)
    return jnp.concatenate([top, top, middle, top, middle, low], axis=1)


def right_parts(value):
    top, middle, low = split(value)
    return jnp.concatenate([top, middle, top, low, middle, top], axis=0)


def eliminate(tiles, tile, offset):
    shape = tiles[0].shape
    row = lax.broadcasted_iota(jnp.int32, shape, 0)
    lane = lax.broadcasted_iota(jnp.int32, shape, 1) - offset
    cols = [
        jnp.broadcast_to(tiles[tile][:, offset + q : offset + q + 1], shape) for q in range(pivots)
    ]
    unit = jnp.where(lane == row, 1.0, 0.0)
    tiles = list(tiles)
    tiles[tile] = jnp.where((lane >= 0) & (lane < pivots), unit, tiles[tile])
    scale = jnp.ones(shape, f32)
    for q in range(pivots):
        here = row == q
        inverse = jnp.broadcast_to(1.0 / cols[q][q : q + 1], shape)
        factor = jnp.where(here, 0.0, cols[q] * inverse)
        scale = jnp.where(here, inverse, scale)
        for p in range(q + 1, pivots):
            cols[p] = cols[p] - factor * jnp.broadcast_to(cols[p][q : q + 1], shape)
        tiles = [part - factor * jnp.broadcast_to(part[q : q + 1], shape) for part in tiles]
    return [part * scale for part in tiles]


def invert(gram_ref):
    size = gram_ref.shape[0]
    starts = range(0, size, lanes)
    for k0 in range(0, size, pivots):
        k1 = k0 + pivots
        k2 = min(k1 + pivots, size)
        tiles = [gram_ref[k0:k2, t : t + lanes] for t in starts]
        tiles = eliminate(tiles, k0 // lanes, k0 % lanes)
        done = jnp.concatenate([part[:pivots] for part in tiles], axis=1)
        right = right_parts(done)
        if k2 > k1:
            for part, t in zip(tiles, starts):
                gram_ref[k1:k2, t : t + lanes] = part[pivots:]

        def update(first, last):
            if first < last:
                rows = gram_ref[first:last]
                lane = lax.broadcasted_iota(jnp.int32, rows.shape, 1)
                base = jnp.where((lane >= k0) & (lane < k1), 0.0, rows)
                gram_ref[first:last] = base - jnp.dot(
                    left_parts(rows[:, k0:k1]), right, preferred_element_type=f32
                )

        update(k2, min(k2 + pivots, size))
        update(k2 + pivots, size)
        update(0, k0)
        gram_ref[k0:k1] = done


def solve_kernel(core_ref, packed_ref, other_ref, gram_c_ref, solved_ref, squares_ref, gram_ref):
    other = other_ref[...]
    peers, rows, ranks = other.shape
    shape = (peers // 2, 2 * rows, ranks)
    gram_b = interleave(
        core_ref[0], packed_ref[:, :rows].reshape(shape), other.reshape(shape)
    ).reshape(ranks, ranks)
    gram_ref[...] = gram_b * gram_c_ref[...]
    invert(gram_ref)
    mine = jnp.sum(packed_ref[:, rows:], axis=0)
    solved = jnp.dot(mine, gram_ref[...], precision=high, preferred_element_type=f32)
    solved_ref[...] = solved
    squares_ref[...] = jnp.sum(solved * solved, axis=0, keepdims=True)


def solve(core, packed, other, gram_c):
    peers, rows, ranks = other.shape
    return pl.pallas_call(
        solve_kernel,
        out_shape=(
            jax.ShapeDtypeStruct((packed.shape[1] - rows, ranks), f32),
            jax.ShapeDtypeStruct((1, ranks), f32),
        ),
        in_specs=[pl.BlockSpec(memory_space=pltpu.SMEM)]
        + [pl.BlockSpec(memory_space=pltpu.VMEM)] * 3,
        scratch_shapes=[pltpu.VMEM((ranks, ranks), f32)],
        compiler_params=pltpu.CompilerParams(vmem_limit_bytes=limit),
        name="solve",
    )(core, packed, other, gram_c)


def finish_kernel(count, squares_ref, solved_ref, factor_ref, scale_ref):
    squares = jnp.sum(squares_ref[...], axis=0)
    scale = jnp.sqrt(squares / count + eps)
    scale_ref[...] = scale
    factor_ref[...] = solved_ref[...] / scale


def finish(squares, solved, count):
    return pl.pallas_call(
        functools.partial(finish_kernel, count),
        out_shape=(
            jax.ShapeDtypeStruct(solved.shape, f32),
            jax.ShapeDtypeStruct((1, solved.shape[1]), f32),
        ),
        compiler_params=pltpu.CompilerParams(vmem_limit_bytes=limit),
        name="finish",
    )(squares, solved)


def local(tensor, factor_b, factor_c):
    depth, rows_i, cols_j = tensor.shape
    n_row, n_col = lax.axis_size("row"), lax.axis_size("col")
    core = (lax.axis_index("row") % 2).astype(jnp.int32)[None]
    chips = n_row // 2
    same_core = [[2 * chip + core for chip in range(chips)] for core in range(2)]
    swap = [(i, i ^ 1) for i in range(n_row)]
    width = factor_b.shape[1]

    copies = jnp.broadcast_to(factor_b.T[None], (chips, width, cols_j))
    mine = lax.all_to_all(copies, "row", 0, 0, axis_index_groups=same_core)
    other = lax.ppermute(mine, "row", swap)
    block, parts = partial_gram(core, mine, other, n_col)
    parts = lax.all_to_all(parts, "col", 0, 0)
    terms, gram_c = mttkrp(tensor, block, factor_c)
    packed = lax.all_to_all(pack(parts, terms), "col", 0, 0)
    other = lax.ppermute(packed[:, : parts.shape[1]], "row", swap)
    solved, squares = solve(core, packed, other, gram_c)
    squares = squares + lax.ppermute(squares, "row", swap)
    same_core = [
        [(2 * chip + core) * n_col + c for chip in range(chips) for c in range(n_col)]
        for core in range(2)
    ]
    copies = jnp.broadcast_to(squares[None], (chips * n_col,) + squares.shape)
    squares = lax.all_to_all(copies, both, 0, 0, axis_index_groups=same_core)
    factor_a, col_scale = finish(squares, solved, rows_i * n_row)
    return (factor_a, col_scale[0])


def solution(mesh):
    return jax.shard_map(
        local,
        mesh=mesh,
        in_specs=(P(None, "row", "col"), P("col", "row"), P()),
        out_specs=(P(both, None), P()),
        check_vma=False,
    )
```

```python
import functools

import jax
import jax.numpy as jnp
from jax import lax
from jax.experimental import pallas as pl
from jax.experimental.pallas import tpu as pltpu
from jax.sharding import PartitionSpec as P

eps = 1e-06
high = lax.Precision.HIGHEST
f32 = jnp.float32
bf16 = jnp.bfloat16
limit = 16 * 1024 * 1024
wide = 52 * 1024 * 1024
pivots = 16
lanes = 128
frames = (4, 12, 16)
both = ("row", "col")
nt = (((1,), (1,)), ((), ()))


def interleave(core, mine, other):
    first = core == 0
    return jnp.concatenate(
        [jnp.where(first, mine, other), jnp.where(first, other, mine)], axis=1
    )


def gram_kernel(core_ref, mine_ref, other_ref, c_ref, block_ref, part_ref, c_out_ref):
    c_out_ref[...] = c_ref[...]
    mine = mine_ref[...]
    count, width, cols_j = mine.shape
    block = interleave(core_ref[0], mine, other_ref[...]).reshape(2 * count * width, cols_j)
    block_ref[...] = block
    part = lax.dot_general(
        mine.reshape(count * width, cols_j), block, nt, precision=high, preferred_element_type=f32
    )
    part_ref[...] = part.reshape(part_ref.shape)


def partial_gram(core, mine, other, factor_c, peers):
    count, width, cols_j = mine.shape
    ranks = 2 * count * width
    return pl.pallas_call(
        gram_kernel,
        out_shape=(
            jax.ShapeDtypeStruct((ranks, cols_j), f32),
            jax.ShapeDtypeStruct((peers, ranks // 2 // peers, ranks), f32),
            jax.ShapeDtypeStruct(factor_c.shape, f32),
        ),
        in_specs=[pl.BlockSpec(memory_space=pltpu.SMEM)]
        + [pl.BlockSpec(memory_space=pltpu.VMEM)] * 3,
        out_specs=[pl.BlockSpec(memory_space=pltpu.VMEM)] * 3,
        compiler_params=pltpu.CompilerParams(vmem_limit_bytes=limit),
        name="gram_part",
    )(core, mine, other, factor_c)


def halves(value):
    top = value.astype(bf16)
    return top, (value - top.astype(f32)).astype(bf16)


def mttkrp_kernel(slab_hbm, block_ref, c_ref, out_ref, gram_c_ref, slab_ref, arrived):
    pieces = []
    first = 0
    for part, count in enumerate(frames):
        here = pl.ds(first, count)
        copy = pltpu.make_async_copy(slab_hbm.at[here], slab_ref.at[here], arrived.at[part])
        pieces.append((copy, range(first, first + count)))
        first += count
    for copy, _ in pieces:
        copy.start()
    c = c_ref[...]
    gram_c_ref[...] = lax.dot_general(
        c, c, (((0,), (0,)), ((), ())), precision=high, preferred_element_type=f32
    )
    top, low = halves(block_ref[...])
    weights = jnp.concatenate([top, low, top], axis=1)
    total = jnp.zeros(out_ref.shape, f32)
    for copy, here in pieces:
        copy.wait()
        for k in here:
            top, low = halves(slab_ref[k])
            product = lax.dot_general(
                jnp.concatenate([top, top, low], axis=1), weights, nt, preferred_element_type=f32
            )
            total += product * c[k : k + 1]
    out_ref[...] = total


def mttkrp(slab, block, factor_c):
    depth, rows_i, cols_j = slab.shape
    ranks = block.shape[0]
    return pl.pallas_call(
        mttkrp_kernel,
        out_shape=(
            jax.ShapeDtypeStruct((rows_i, ranks), f32),
            jax.ShapeDtypeStruct((ranks, ranks), f32),
        ),
        in_specs=[pl.BlockSpec(memory_space=pl.ANY)]
        + [pl.BlockSpec(memory_space=pltpu.VMEM)] * 2,
        scratch_shapes=[
            pltpu.VMEM(slab.shape, f32),
            pltpu.SemaphoreType.DMA((len(frames),)),
        ],
        compiler_params=pltpu.CompilerParams(vmem_limit_bytes=wide),
        cost_estimate=pl.CostEstimate(
            flops=6 * depth * rows_i * cols_j * ranks,
            bytes_accessed=4 * depth * rows_i * cols_j,
            transcendentals=0,
        ),
        name="mttkrp",
    )(slab, block, factor_c)


def pack_kernel(parts_ref, terms_ref, out_ref):
    rows = parts_ref.shape[1]
    total = jnp.sum(parts_ref[...], axis=0)
    out_ref[:, :rows] = jnp.broadcast_to(total[None], parts_ref.shape)
    out_ref[:, rows:] = terms_ref[...].reshape(out_ref[:, rows:].shape)


def pack(parts, terms):
    peers, rows, ranks = parts.shape
    return pl.pallas_call(
        pack_kernel,
        out_shape=jax.ShapeDtypeStruct((peers, rows + terms.shape[0] // peers, ranks), f32),
        compiler_params=pltpu.CompilerParams(vmem_limit_bytes=limit),
        name="pack",
    )(parts, terms)


def split(value):
    top = value.astype(bf16)
    rest = value - top.astype(f32)
    middle = rest.astype(bf16)
    return top, middle, (rest - middle.astype(f32)).astype(bf16)


def left_parts(value):
    top, middle, low = split(value)
    return jnp.concatenate([top, top, middle, top, middle, low], axis=0)


def right_parts(value):
    top, middle, low = split(value)
    return jnp.concatenate([top, middle, top, low, middle, top], axis=0)


def spread(block, offset):
    return [
        jnp.broadcast_to(block[:, offset + q : offset + q + 1], block.shape) for q in range(pivots)
    ]


def over_rows(tile, q):
    return jnp.broadcast_to(tile[q : q + 1], tile.shape)


def eliminate(tiles, tile, offset):
    shape = tiles[0].shape
    row = lax.broadcasted_iota(jnp.int32, shape, 0)
    lane = lax.broadcasted_iota(jnp.int32, shape, 1) - offset
    cols = spread(tiles[tile], offset)
    tiles = list(tiles)
    unit = jnp.where(lane == row, 1.0, 0.0)
    tiles[tile] = jnp.where((lane >= 0) & (lane < pivots), unit, tiles[tile])
    scale = jnp.ones(shape, f32)
    for q in range(pivots):
        here = row == q
        if q + 1 < pivots:
            change = jnp.where(here, 0.0, cols[q] * over_rows(cols[q + 1], q))
        inverse = jnp.broadcast_to(1.0 / cols[q][q : q + 1], shape)
        factor = jnp.where(here, 0.0, cols[q] * inverse)
        scale = jnp.where(here, inverse, scale)
        if q + 1 < pivots:
            cols[q + 1] = cols[q + 1] - change * inverse
        for p in range(q + 2, pivots):
            cols[p] = cols[p] - factor * over_rows(cols[p], q)
        tiles = [part - factor * over_rows(part, q) for part in tiles]
    return [part * scale for part in tiles]


def invert(gram_ref):
    size = gram_ref.shape[0]
    starts = range(0, size, lanes)
    lane = lax.broadcasted_iota(jnp.int32, (pivots, lanes), 1)
    for k0 in range(0, size, pivots):
        k1 = k0 + pivots
        k2 = min(k1 + pivots, size)
        tile, offset = k0 // lanes, k0 % lanes

        def without_block(rows, t):
            here = lax.broadcasted_iota(jnp.int32, rows.shape, 1) - offset
            return jnp.where((here >= 0) & (here < pivots), 0.0, rows) if t == tile else rows

        head = [gram_ref[k0:k1, t : t + lanes] for t in starts]
        signed = [jnp.where(lane < k0 - t, -part, part) for part, t in zip(head, starts)]
        left = left_parts(jnp.concatenate(signed, axis=1))
        if k2 > k1:
            ahead = spread(gram_ref[k1:k2, tile * lanes : (tile + 1) * lanes], offset)
        done = eliminate(head, tile, offset)
        for t, part in enumerate(done):
            here = slice(t * lanes, (t + 1) * lanes)
            if k2 > k1:
                sums = [ahead[q] * over_rows(part, q) for q in range(4)]
                for q in range(4, pivots):
                    sums[q % 4] = sums[q % 4] + ahead[q] * over_rows(part, q)
                change = (sums[0] + sums[1]) + (sums[2] + sums[3])
                gram_ref[k1:k2, here] = without_block(gram_ref[k1:k2, here], t) - change
        update = lax.dot_general(
            left, right_parts(jnp.concatenate(done, axis=1)), (((0,), (0,)), ((), ())),
            preferred_element_type=f32,
        )
        for t, part in enumerate(done):
            here = slice(t * lanes, (t + 1) * lanes)
            for first, last in ((k2, size), (0, k0)):
                if first < last:
                    rows = without_block(gram_ref[first:last, here], t)
                    gram_ref[first:last, here] = rows - update[first:last, here]
            gram_ref[k0:k1, here] = part


def solve_kernel(core_ref, packed_ref, other_ref, gram_c_ref, solved_ref, squares_ref, gram_ref):
    other = other_ref[...]
    peers, rows, ranks = other.shape
    shape = (peers // 2, 2 * rows, ranks)
    gram_b = interleave(
        core_ref[0], packed_ref[:, :rows].reshape(shape), other.reshape(shape)
    ).reshape(ranks, ranks)
    gram_ref[...] = gram_b * gram_c_ref[...]
    invert(gram_ref)
    mine = jnp.sum(packed_ref[:, rows:], axis=0)
    solved = jnp.dot(mine, gram_ref[...], precision=high, preferred_element_type=f32)
    solved_ref[...] = solved
    squares_ref[...] = jnp.sum(solved * solved, axis=0, keepdims=True)


def solve(core, packed, other, gram_c):
    peers, rows, ranks = other.shape
    return pl.pallas_call(
        solve_kernel,
        out_shape=(
            jax.ShapeDtypeStruct((packed.shape[1] - rows, ranks), f32),
            jax.ShapeDtypeStruct((1, ranks), f32),
        ),
        in_specs=[pl.BlockSpec(memory_space=pltpu.SMEM)]
        + [pl.BlockSpec(memory_space=pltpu.VMEM)] * 3,
        scratch_shapes=[pltpu.VMEM((ranks, ranks), f32)],
        compiler_params=pltpu.CompilerParams(vmem_limit_bytes=limit),
        name="solve",
    )(core, packed, other, gram_c)


def finish_kernel(count, squares_ref, solved_ref, factor_ref, scale_ref):
    squares = jnp.sum(squares_ref[...], axis=0)
    scale = jnp.sqrt(squares / count + eps)
    scale_ref[...] = scale
    factor_ref[...] = solved_ref[...] / scale


def finish(squares, solved, count):
    return pl.pallas_call(
        functools.partial(finish_kernel, count),
        out_shape=(
            jax.ShapeDtypeStruct(solved.shape, f32),
            jax.ShapeDtypeStruct((1, solved.shape[1]), f32),
        ),
        compiler_params=pltpu.CompilerParams(vmem_limit_bytes=limit),
        name="finish",
    )(squares, solved)


def local(tensor, factor_b, factor_c):
    depth, rows_i, cols_j = tensor.shape
    n_row, n_col = lax.axis_size("row"), lax.axis_size("col")
    core = (lax.axis_index("row") % 2).astype(jnp.int32)[None]
    chips = n_row // 2
    same_core = [[2 * chip + core for chip in range(chips)] for core in range(2)]
    swap = [(i, i ^ 1) for i in range(n_row)]
    width = factor_b.shape[1]

    copies = jnp.broadcast_to(factor_b.T[None], (chips, width, cols_j))
    mine = lax.all_to_all(copies, "row", 0, 0, axis_index_groups=same_core)
    other = lax.ppermute(mine, "row", swap)
    block, parts, factor_c = partial_gram(core, mine, other, factor_c, n_col)
    parts = lax.all_to_all(parts, "col", 0, 0)
    terms, gram_c = mttkrp(tensor, block, factor_c)
    packed = lax.all_to_all(pack(parts, terms), "col", 0, 0)
    other = lax.ppermute(packed[:, : parts.shape[1]], "row", swap)
    solved, squares = solve(core, packed, other, gram_c)
    squares = squares + lax.ppermute(squares, "row", swap)
    same_core = [
        [(2 * chip + core) * n_col + c for chip in range(chips) for c in range(n_col)]
        for core in range(2)
    ]
    copies = jnp.broadcast_to(squares[None], (chips * n_col,) + squares.shape)
    squares = lax.all_to_all(copies, both, 0, 0, axis_index_groups=same_core)
    factor_a, col_scale = finish(squares, solved, rows_i * n_row)
    return (factor_a, col_scale[0])


def solution(mesh):
    return jax.shard_map(
        local,
        mesh=mesh,
        in_specs=(P(None, "row", "col"), P("col", "row"), P()),
        out_specs=(P(both, None), P()),
        check_vma=False,
    )
```

```python
import functools

import jax
import jax.numpy as jnp
from jax import lax
from jax.experimental import pallas as pl
from jax.experimental.pallas import tpu as pltpu
from jax.sharding import PartitionSpec as P

eps = 1e-06
high = lax.Precision.HIGHEST
f32 = jnp.float32
bf16 = jnp.bfloat16
limit = 16 * 1024 * 1024
wide = 52 * 1024 * 1024
beside = 10**10
pivots = 16
lanes = 128
frames = (4, 12, 16)
both = ("row", "col")
nt = (((1,), (1,)), ((), ()))


def gram_kernel(mine_ref, other_ref, block_ref, part_ref):
    mine = mine_ref[...].reshape(part_ref.shape[0] * part_ref.shape[1], block_ref.shape[1])
    block_ref[: mine.shape[0]] = mine
    block_ref[mine.shape[0] :] = other_ref[...].reshape(mine.shape)
    part = lax.dot_general(mine, block_ref[...], nt, precision=high, preferred_element_type=f32)
    part_ref[...] = part.reshape(part_ref.shape)


def partial_gram(mine, other, peers):
    count, width, cols_j = mine.shape
    ranks = 2 * count * width
    return pl.pallas_call(
        gram_kernel,
        out_shape=(
            jax.ShapeDtypeStruct((ranks, cols_j), f32),
            jax.ShapeDtypeStruct((peers, ranks // 2 // peers, ranks), f32),
        ),
        compiler_params=pltpu.CompilerParams(vmem_limit_bytes=limit),
        cost_estimate=pl.CostEstimate(
            flops=beside, bytes_accessed=8 * ranks * cols_j, transcendentals=0
        ),
        name="gram_part",
    )(mine, other)


def own_first(core, value):
    front, back = value[:, :lanes], value[:, lanes:]
    lane = lax.broadcasted_iota(jnp.int32, front.shape, 1)
    tiles = []
    for whose in (core, 1 - core):
        index = 32 * (lane // 16 % 4) + 16 * whose + lane % 16
        low, top = (jnp.take_along_axis(part, index, axis=1) for part in (front, back))
        tiles.append(jnp.where(lane < lanes // 2, low, top))
    return jnp.concatenate(tiles, axis=1)


def by_turns(core, value):
    own, other = value[:, :lanes], value[:, lanes:]
    lane = lax.broadcasted_iota(jnp.int32, own.shape, 1)
    tiles = []
    for t in range(2):
        index = 16 * (4 * t + lane // 32) + lane % 16
        ours, theirs = (jnp.take_along_axis(part, index, axis=1) for part in (own, other))
        tiles.append(jnp.where(lane // 16 % 2 == core, ours, theirs))
    return jnp.concatenate(tiles, axis=1)


def halves(value):
    top = value.astype(bf16)
    return top, (value - top.astype(f32)).astype(bf16)


def mttkrp_kernel(core_ref, slab_hbm, block_ref, c_ref, out_ref, gram_c_ref, slab_ref, arrived):
    pieces = []
    first = 0
    for part, count in enumerate(frames):
        here = pl.ds(first, count)
        copy = pltpu.make_async_copy(slab_hbm.at[here], slab_ref.at[here], arrived.at[part])
        pieces.append((copy, range(first, first + count)))
        first += count
    for copy, _ in pieces:
        copy.start()
    c = own_first(core_ref[0], c_ref[...])
    gram_c_ref[...] = lax.dot_general(
        c, c, (((0,), (0,)), ((), ())), precision=high, preferred_element_type=f32
    )
    top, low = halves(block_ref[...])
    weights = jnp.concatenate([top, low, top], axis=1)
    total = jnp.zeros(out_ref.shape, f32)
    for copy, here in pieces:
        copy.wait()
        for k in here:
            top, low = halves(slab_ref[k])
            product = lax.dot_general(
                jnp.concatenate([top, top, low], axis=1), weights, nt, preferred_element_type=f32
            )
            total += product * c[k : k + 1]
    out_ref[...] = total


def mttkrp(core, slab, block, factor_c):
    depth, rows_i, cols_j = slab.shape
    ranks = block.shape[0]
    return pl.pallas_call(
        mttkrp_kernel,
        out_shape=(
            jax.ShapeDtypeStruct((rows_i, ranks), f32),
            jax.ShapeDtypeStruct((ranks, ranks), f32),
        ),
        in_specs=[pl.BlockSpec(memory_space=pltpu.SMEM), pl.BlockSpec(memory_space=pl.ANY)]
        + [pl.BlockSpec(memory_space=pltpu.VMEM)] * 2,
        scratch_shapes=[
            pltpu.VMEM(slab.shape, f32),
            pltpu.SemaphoreType.DMA((len(frames),)),
        ],
        compiler_params=pltpu.CompilerParams(vmem_limit_bytes=wide),
        cost_estimate=pl.CostEstimate(
            flops=6 * depth * rows_i * cols_j * ranks,
            bytes_accessed=4 * depth * rows_i * cols_j,
            transcendentals=0,
        ),
        name="mttkrp",
    )(core, slab, block, factor_c)


def pack_kernel(parts_ref, terms_ref, out_ref):
    rows = parts_ref.shape[1]
    total = jnp.sum(parts_ref[...], axis=0)
    out_ref[:, :rows] = jnp.broadcast_to(total[None], parts_ref.shape)
    out_ref[:, rows:] = terms_ref[...].reshape(out_ref[:, rows:].shape)


def pack(parts, terms):
    peers, rows, ranks = parts.shape
    return pl.pallas_call(
        pack_kernel,
        out_shape=jax.ShapeDtypeStruct((peers, rows + terms.shape[0] // peers, ranks), f32),
        compiler_params=pltpu.CompilerParams(vmem_limit_bytes=limit),
        name="pack",
    )(parts, terms)


def split(value):
    top = value.astype(bf16)
    rest = value - top.astype(f32)
    middle = rest.astype(bf16)
    return top, middle, (rest - middle.astype(f32)).astype(bf16)


def left_parts(value):
    top, middle, low = split(value)
    return jnp.concatenate([top, top, middle, top, middle, low], axis=0)


def right_parts(value):
    top, middle, low = split(value)
    return jnp.concatenate([top, middle, top, low, middle, top], axis=0)


def spread(block, offset):
    return [
        jnp.broadcast_to(block[:, offset + q : offset + q + 1], block.shape) for q in range(pivots)
    ]


def over_rows(tile, q):
    return jnp.broadcast_to(tile[q : q + 1], tile.shape)


def eliminate(tiles, tile, offset):
    shape = tiles[0].shape
    row = lax.broadcasted_iota(jnp.int32, shape, 0)
    lane = lax.broadcasted_iota(jnp.int32, shape, 1) - offset
    cols = spread(tiles[tile], offset)
    tiles = list(tiles)
    unit = jnp.where(lane == row, 1.0, 0.0)
    tiles[tile] = jnp.where((lane >= 0) & (lane < pivots), unit, tiles[tile])
    scale = jnp.ones(shape, f32)
    for q in range(pivots):
        here = row == q
        if q + 1 < pivots:
            change = jnp.where(here, 0.0, cols[q] * over_rows(cols[q + 1], q))
        inverse = jnp.broadcast_to(1.0 / cols[q][q : q + 1], shape)
        factor = jnp.where(here, 0.0, cols[q] * inverse)
        scale = jnp.where(here, inverse, scale)
        if q + 1 < pivots:
            cols[q + 1] = cols[q + 1] - change * inverse
        for p in range(q + 2, pivots):
            cols[p] = cols[p] - factor * over_rows(cols[p], q)
        tiles = [part - factor * over_rows(part, q) for part in tiles]
    return [part * scale for part in tiles]


def invert(gram_ref, begin, end):
    size, ranks = gram_ref.shape
    starts = range(0, ranks, lanes)
    lane = lax.broadcasted_iota(jnp.int32, (pivots, lanes), 1)
    for k0 in range(begin, end, pivots):
        k1 = k0 + pivots
        k2 = min(k1 + pivots, size)
        tile, offset = k0 // lanes, k0 % lanes

        def without_block(rows, t):
            here = lax.broadcasted_iota(jnp.int32, rows.shape, 1) - offset
            return jnp.where((here >= 0) & (here < pivots), 0.0, rows) if t == tile else rows

        head = [gram_ref[k0:k1, t : t + lanes] for t in starts]
        signed = [jnp.where(lane < k0 - t, -part, part) for part, t in zip(head, starts)]
        left = left_parts(jnp.concatenate(signed[: size // lanes], axis=1))
        if k2 > k1:
            ahead = spread(gram_ref[k1:k2, tile * lanes : (tile + 1) * lanes], offset)
        done = eliminate(head, tile, offset)
        for t, part in enumerate(done):
            here = slice(t * lanes, (t + 1) * lanes)
            if k2 > k1:
                sums = [ahead[q] * over_rows(part, q) for q in range(4)]
                for q in range(4, pivots):
                    sums[q % 4] = sums[q % 4] + ahead[q] * over_rows(part, q)
                change = (sums[0] + sums[1]) + (sums[2] + sums[3])
                gram_ref[k1:k2, here] = without_block(gram_ref[k1:k2, here], t) - change
        update = lax.dot_general(
            left, right_parts(jnp.concatenate(done, axis=1)), (((0,), (0,)), ((), ())),
            preferred_element_type=f32,
        )
        for t, part in enumerate(done):
            here = slice(t * lanes, (t + 1) * lanes)
            for first, last in ((k2, size), (0, k0)):
                if first < last:
                    rows = without_block(gram_ref[first:last, here], t)
                    gram_ref[first:last, here] = rows - update[first:last, here]
            gram_ref[k0:k1, here] = part


def first_kernel(packed_ref, gram_c_ref, own_ref, change_ref):
    half, ranks = own_ref.shape
    rows = half // packed_ref.shape[0]
    own = packed_ref[:, :rows].reshape(half, ranks) * gram_c_ref[:half]
    own_ref[...] = own
    left = left_parts(own[:, half:])
    invert(own_ref, 0, half)
    change_ref[...] = lax.dot_general(
        left, right_parts(own_ref[...]), (((0,), (0,)), ((), ())), preferred_element_type=f32
    )


def first_half(packed, gram_c):
    half = jax.ShapeDtypeStruct((gram_c.shape[0] // 2, gram_c.shape[1]), f32)
    return pl.pallas_call(
        first_kernel,
        out_shape=(half, half),
        compiler_params=pltpu.CompilerParams(vmem_limit_bytes=limit),
        cost_estimate=pl.CostEstimate(
            flops=beside, bytes_accessed=packed.size * 4, transcendentals=0
        ),
        name="first_half",
    )(packed, gram_c)


def solve_kernel(
    core_ref, own_ref, change_ref, packed_ref, other_ref, gram_c_ref, solved_ref, squares_ref, gram_ref
):
    half, ranks = own_ref.shape
    rows = other_ref.shape[1]
    gram_ref[:half] = own_ref[...]
    other = other_ref[...].reshape(half, ranks)[:, :half] * gram_c_ref[half:, half:]
    gram_ref[half:, :half] = -change_ref[:, :half]
    gram_ref[half:, half:] = other - change_ref[:, half:]
    invert(gram_ref, half, ranks)
    mine = jnp.sum(packed_ref[:, rows:], axis=0)
    solved = jnp.dot(mine, gram_ref[...], precision=high, preferred_element_type=f32)
    solved = by_turns(core_ref[0], solved)
    solved_ref[...] = solved
    squares_ref[...] = jnp.sum(solved * solved, axis=0, keepdims=True)


def solve(core, own, change, packed, other, gram_c):
    peers, rows, ranks = other.shape
    return pl.pallas_call(
        solve_kernel,
        out_shape=(
            jax.ShapeDtypeStruct((packed.shape[1] - rows, ranks), f32),
            jax.ShapeDtypeStruct((1, ranks), f32),
        ),
        in_specs=[pl.BlockSpec(memory_space=pltpu.SMEM)]
        + [pl.BlockSpec(memory_space=pltpu.VMEM)] * 5,
        scratch_shapes=[pltpu.VMEM((ranks, ranks), f32)],
        compiler_params=pltpu.CompilerParams(vmem_limit_bytes=limit),
        name="solve",
    )(core, own, change, packed, other, gram_c)


def finish_kernel(count, squares_ref, solved_ref, factor_ref, scale_ref):
    squares = jnp.sum(squares_ref[...], axis=0)
    scale = jnp.sqrt(squares / count + eps)
    scale_ref[...] = scale
    factor_ref[...] = solved_ref[...] / scale


def finish(squares, solved, count):
    return pl.pallas_call(
        functools.partial(finish_kernel, count),
        out_shape=(
            jax.ShapeDtypeStruct(solved.shape, f32),
            jax.ShapeDtypeStruct((1, solved.shape[1]), f32),
        ),
        compiler_params=pltpu.CompilerParams(vmem_limit_bytes=limit),
        name="finish",
    )(squares, solved)


def local(tensor, factor_b, factor_c):
    depth, rows_i, cols_j = tensor.shape
    n_row, n_col = lax.axis_size("row"), lax.axis_size("col")
    core = (lax.axis_index("row") % 2).astype(jnp.int32)[None]
    chips = n_row // 2
    same_core = [[2 * chip + core for chip in range(chips)] for core in range(2)]
    swap = [(i, i ^ 1) for i in range(n_row)]
    width = factor_b.shape[1]

    copies = jnp.broadcast_to(factor_b.T[None], (chips, width, cols_j))
    mine = lax.all_to_all(copies, "row", 0, 0, axis_index_groups=same_core)
    other = lax.ppermute(mine, "row", swap)
    block, parts = partial_gram(mine, other, n_col)
    parts = lax.all_to_all(parts, "col", 0, 0)
    terms, gram_c = mttkrp(core, tensor, block, factor_c)
    packed = lax.all_to_all(pack(parts, terms), "col", 0, 0)
    other = lax.ppermute(packed[:, : parts.shape[1]], "row", swap)
    own, change = first_half(packed, gram_c)
    solved, squares = solve(core, own, change, packed, other, gram_c)
    squares = squares + lax.ppermute(squares, "row", swap)
    same_core = [
        [(2 * chip + core) * n_col + c for chip in range(chips) for c in range(n_col)]
        for core in range(2)
    ]
    copies = jnp.broadcast_to(squares[None], (chips * n_col,) + squares.shape)
    squares = lax.all_to_all(copies, both, 0, 0, axis_index_groups=same_core)
    factor_a, col_scale = finish(squares, solved, rows_i * n_row)
    return (factor_a, col_scale[0])


def solution(mesh):
    return jax.shard_map(
        local,
        mesh=mesh,
        in_specs=(P(None, "row", "col"), P("col", "row"), P()),
        out_specs=(P(both, None), P()),
        check_vma=False,
    )
```

```python
import functools

import jax
import jax.numpy as jnp
from jax import lax
from jax.experimental import pallas as pl
from jax.experimental.pallas import tpu as pltpu
from jax.sharding import PartitionSpec as P

eps = 1e-06
high = lax.Precision.HIGHEST
f32 = jnp.float32
bf16 = jnp.bfloat16
limit = 16 * 1024 * 1024
wide = 52 * 1024 * 1024
beside = 10**10
pivots = 16
lanes = 128
frames = (4, 12, 16)
both = ("row", "col")
nt = (((1,), (1,)), ((), ()))


def rank_gram(left, right):
    return lax.dot_general(left, right, nt, precision=high, preferred_element_type=f32)


def own_kernel(mine_ref, own_ref):
    mine = mine_ref[...].reshape(own_ref.shape[0], mine_ref.shape[2])
    own_ref[...] = rank_gram(mine, mine)


def own_gram(mine):
    half = mine.shape[0] * mine.shape[1]
    return pl.pallas_call(
        own_kernel,
        out_shape=jax.ShapeDtypeStruct((half, half), f32),
        compiler_params=pltpu.CompilerParams(vmem_limit_bytes=limit),
        cost_estimate=pl.CostEstimate(
            flops=beside, bytes_accessed=4 * mine.size, transcendentals=0
        ),
        name="gram_own",
    )(mine)


def gram_kernel(mine_ref, other_ref, own_ref, block_ref, part_ref):
    half = own_ref.shape[0]
    mine = mine_ref[...].reshape(half, block_ref.shape[1])
    other = other_ref[...].reshape(mine.shape)
    block_ref[:half] = mine
    block_ref[half:] = other
    part_ref[:, :, :half] = own_ref[...].reshape(part_ref.shape[:2] + (half,))
    part_ref[:, :, half:] = rank_gram(mine, other).reshape(part_ref.shape[:2] + (half,))


def partial_gram(mine, other, own, peers):
    count, width, cols_j = mine.shape
    ranks = 2 * count * width
    return pl.pallas_call(
        gram_kernel,
        out_shape=(
            jax.ShapeDtypeStruct((ranks, cols_j), f32),
            jax.ShapeDtypeStruct((peers, ranks // 2 // peers, ranks), f32),
        ),
        compiler_params=pltpu.CompilerParams(vmem_limit_bytes=limit),
        cost_estimate=pl.CostEstimate(
            flops=beside, bytes_accessed=8 * ranks * cols_j, transcendentals=0
        ),
        name="gram_part",
    )(mine, other, own)


def own_first(core, value):
    front, back = value[:, :lanes], value[:, lanes:]
    lane = lax.broadcasted_iota(jnp.int32, front.shape, 1)
    tiles = []
    for whose in (core, 1 - core):
        index = 32 * (lane // 16 % 4) + 16 * whose + lane % 16
        low, top = (jnp.take_along_axis(part, index, axis=1) for part in (front, back))
        tiles.append(jnp.where(lane < lanes // 2, low, top))
    return jnp.concatenate(tiles, axis=1)


def by_turns(core, value):
    own, other = value[:, :lanes], value[:, lanes:]
    lane = lax.broadcasted_iota(jnp.int32, own.shape, 1)
    tiles = []
    for t in range(2):
        index = 16 * (4 * t + lane // 32) + lane % 16
        ours, theirs = (jnp.take_along_axis(part, index, axis=1) for part in (own, other))
        tiles.append(jnp.where(lane // 16 % 2 == core, ours, theirs))
    return jnp.concatenate(tiles, axis=1)


def halves(value):
    top = value.astype(bf16)
    return top, (value - top.astype(f32)).astype(bf16)


def mttkrp_kernel(core_ref, slab_hbm, block_ref, c_ref, out_ref, gram_c_ref, slab_ref, arrived):
    pieces = []
    first = 0
    for part, count in enumerate(frames):
        here = pl.ds(first, count)
        copy = pltpu.make_async_copy(slab_hbm.at[here], slab_ref.at[here], arrived.at[part])
        pieces.append((copy, range(first, first + count)))
        first += count
    for copy, _ in pieces:
        copy.start()
    c = own_first(core_ref[0], c_ref[...])
    gram_c_ref[...] = lax.dot_general(
        c, c, (((0,), (0,)), ((), ())), precision=high, preferred_element_type=f32
    )
    top, low = halves(block_ref[...])
    weights = jnp.concatenate([top, low, top], axis=1)
    total = jnp.zeros(out_ref.shape, f32)
    for copy, here in pieces:
        copy.wait()
        for k in here:
            top, low = halves(slab_ref[k])
            product = lax.dot_general(
                jnp.concatenate([top, top, low], axis=1), weights, nt, preferred_element_type=f32
            )
            total += product * c[k : k + 1]
    out_ref[...] = total


def mttkrp(core, slab, block, factor_c):
    depth, rows_i, cols_j = slab.shape
    ranks = block.shape[0]
    return pl.pallas_call(
        mttkrp_kernel,
        out_shape=(
            jax.ShapeDtypeStruct((rows_i, ranks), f32),
            jax.ShapeDtypeStruct((ranks, ranks), f32),
        ),
        in_specs=[pl.BlockSpec(memory_space=pltpu.SMEM), pl.BlockSpec(memory_space=pl.ANY)]
        + [pl.BlockSpec(memory_space=pltpu.VMEM)] * 2,
        scratch_shapes=[
            pltpu.VMEM(slab.shape, f32),
            pltpu.SemaphoreType.DMA((len(frames),)),
        ],
        compiler_params=pltpu.CompilerParams(vmem_limit_bytes=wide),
        cost_estimate=pl.CostEstimate(
            flops=6 * depth * rows_i * cols_j * ranks,
            bytes_accessed=4 * depth * rows_i * cols_j,
            transcendentals=0,
        ),
        name="mttkrp",
    )(core, slab, block, factor_c)


def pack_kernel(parts_ref, terms_ref, out_ref):
    rows = parts_ref.shape[1]
    total = jnp.sum(parts_ref[...], axis=0)
    out_ref[:, :rows] = jnp.broadcast_to(total[None], parts_ref.shape)
    out_ref[:, rows:] = terms_ref[...].reshape(out_ref[:, rows:].shape)


def pack(parts, terms):
    peers, rows, ranks = parts.shape
    return pl.pallas_call(
        pack_kernel,
        out_shape=jax.ShapeDtypeStruct((peers, rows + terms.shape[0] // peers, ranks), f32),
        compiler_params=pltpu.CompilerParams(vmem_limit_bytes=limit),
        name="pack",
    )(parts, terms)


def split(value):
    top = value.astype(bf16)
    rest = value - top.astype(f32)
    middle = rest.astype(bf16)
    return top, middle, (rest - middle.astype(f32)).astype(bf16)


def left_parts(value):
    top, middle, low = split(value)
    return jnp.concatenate([top, top, middle, top, middle, low], axis=0)


def right_parts(value):
    top, middle, low = split(value)
    return jnp.concatenate([top, middle, top, low, middle, top], axis=0)


def spread(block, offset):
    return [
        jnp.broadcast_to(block[:, offset + q : offset + q + 1], block.shape) for q in range(pivots)
    ]


def over_rows(tile, q):
    return jnp.broadcast_to(tile[q : q + 1], tile.shape)


def eliminate(tiles, tile, offset):
    shape = tiles[0].shape
    row = lax.broadcasted_iota(jnp.int32, shape, 0)
    lane = lax.broadcasted_iota(jnp.int32, shape, 1) - offset
    cols = spread(tiles[tile], offset)
    tiles = list(tiles)
    unit = jnp.where(lane == row, 1.0, 0.0)
    tiles[tile] = jnp.where((lane >= 0) & (lane < pivots), unit, tiles[tile])
    scale = jnp.ones(shape, f32)
    pivot = over_rows(cols[0], 0)
    for q in range(pivots):
        here = row == q
        inverse = 1.0 / pivot
        near = range(q + 1, min(q + 1 + 1, pivots))
        masked = jnp.where(here, 0.0, cols[q])
        change = [masked * over_rows(cols[p], q) for p in near]
        if q + 1 < pivots:
            pivot = over_rows(cols[q + 1], q + 1) - over_rows(change[0], q + 1) * inverse
        factor = masked * inverse
        scale = jnp.where(here, inverse, scale)
        for p, term in zip(near, change):
            cols[p] = cols[p] - term * inverse
        for p in range(q + 1 + 1, pivots):
            cols[p] = cols[p] - factor * over_rows(cols[p], q)
        tiles = [part - factor * over_rows(part, q) for part in tiles]
    return [part * scale for part in tiles]


def invert(gram_ref, begin, end):
    size, ranks = gram_ref.shape
    starts = range(0, ranks, lanes)
    lane = lax.broadcasted_iota(jnp.int32, (pivots, lanes), 1)
    for k0 in range(begin, end, pivots):
        k1 = k0 + pivots
        k2 = min(k1 + pivots, size)
        tile, offset = k0 // lanes, k0 % lanes

        def without_block(rows, t):
            here = lax.broadcasted_iota(jnp.int32, rows.shape, 1) - offset
            return jnp.where((here >= 0) & (here < pivots), 0.0, rows) if t == tile else rows

        head = [gram_ref[k0:k1, t : t + lanes] for t in starts]
        signed = [jnp.where(lane < k0 - t, -part, part) for part, t in zip(head, starts)]
        left = left_parts(jnp.concatenate(signed[: size // lanes], axis=1))
        if k2 > k1:
            ahead = spread(gram_ref[k1:k2, tile * lanes : (tile + 1) * lanes], offset)
        done = eliminate(head, tile, offset)
        for t, part in enumerate(done):
            here = slice(t * lanes, (t + 1) * lanes)
            if k2 > k1:
                sums = [ahead[q] * over_rows(part, q) for q in range(4)]
                for q in range(4, pivots):
                    sums[q % 4] = sums[q % 4] + ahead[q] * over_rows(part, q)
                change = (sums[0] + sums[1]) + (sums[2] + sums[3])
                gram_ref[k1:k2, here] = without_block(gram_ref[k1:k2, here], t) - change
        update = lax.dot_general(
            left, right_parts(jnp.concatenate(done, axis=1)), (((0,), (0,)), ((), ())),
            preferred_element_type=f32,
        )
        for t, part in enumerate(done):
            here = slice(t * lanes, (t + 1) * lanes)
            for first, last in ((k2, size), (0, k0)):
                if first < last:
                    rows = without_block(gram_ref[first:last, here], t)
                    gram_ref[first:last, here] = rows - update[first:last, here]
            gram_ref[k0:k1, here] = part


def first_kernel(packed_ref, gram_c_ref, own_ref, change_ref):
    half, ranks = own_ref.shape
    rows = half // packed_ref.shape[0]
    own = packed_ref[:, :rows].reshape(half, ranks) * gram_c_ref[:half]
    own_ref[...] = own
    left = left_parts(own[:, half:])
    invert(own_ref, 0, half)
    change_ref[...] = lax.dot_general(
        left, right_parts(own_ref[...]), (((0,), (0,)), ((), ())), preferred_element_type=f32
    )


def first_half(packed, gram_c):
    half = jax.ShapeDtypeStruct((gram_c.shape[0] // 2, gram_c.shape[1]), f32)
    return pl.pallas_call(
        first_kernel,
        out_shape=(half, half),
        compiler_params=pltpu.CompilerParams(vmem_limit_bytes=limit),
        cost_estimate=pl.CostEstimate(
            flops=beside, bytes_accessed=packed.size * 4, transcendentals=0
        ),
        name="first_half",
    )(packed, gram_c)


def solve_kernel(
    core_ref, own_ref, change_ref, packed_ref, other_ref, gram_c_ref, solved_ref, squares_ref, gram_ref
):
    half, ranks = own_ref.shape
    rows = other_ref.shape[1]
    gram_ref[:half] = own_ref[...]
    other = other_ref[...].reshape(half, ranks)[:, :half] * gram_c_ref[half:, half:]
    gram_ref[half:, :half] = -change_ref[:, :half]
    gram_ref[half:, half:] = other - change_ref[:, half:]
    invert(gram_ref, half, ranks)
    mine = jnp.sum(packed_ref[:, rows:], axis=0)
    solved = jnp.dot(mine, gram_ref[...], precision=high, preferred_element_type=f32)
    solved = by_turns(core_ref[0], solved)
    solved_ref[...] = solved
    squares_ref[...] = jnp.sum(solved * solved, axis=0, keepdims=True)


def solve(core, own, change, packed, other, gram_c):
    peers, rows, ranks = other.shape
    return pl.pallas_call(
        solve_kernel,
        out_shape=(
            jax.ShapeDtypeStruct((packed.shape[1] - rows, ranks), f32),
            jax.ShapeDtypeStruct((1, ranks), f32),
        ),
        in_specs=[pl.BlockSpec(memory_space=pltpu.SMEM)]
        + [pl.BlockSpec(memory_space=pltpu.VMEM)] * 5,
        scratch_shapes=[pltpu.VMEM((ranks, ranks), f32)],
        compiler_params=pltpu.CompilerParams(vmem_limit_bytes=limit),
        name="solve",
    )(core, own, change, packed, other, gram_c)


def finish_kernel(count, squares_ref, solved_ref, factor_ref, scale_ref):
    squares = jnp.sum(squares_ref[...], axis=0)
    scale = jnp.sqrt(squares / count + eps)
    scale_ref[...] = scale
    factor_ref[...] = solved_ref[...] / scale


def finish(squares, solved, count):
    return pl.pallas_call(
        functools.partial(finish_kernel, count),
        out_shape=(
            jax.ShapeDtypeStruct(solved.shape, f32),
            jax.ShapeDtypeStruct((1, solved.shape[1]), f32),
        ),
        compiler_params=pltpu.CompilerParams(vmem_limit_bytes=limit),
        name="finish",
    )(squares, solved)


def local(tensor, factor_b, factor_c):
    depth, rows_i, cols_j = tensor.shape
    n_row, n_col = lax.axis_size("row"), lax.axis_size("col")
    core = (lax.axis_index("row") % 2).astype(jnp.int32)[None]
    chips = n_row // 2
    same_core = [[2 * chip + core for chip in range(chips)] for core in range(2)]
    swap = [(i, i ^ 1) for i in range(n_row)]
    width = factor_b.shape[1]

    copies = jnp.broadcast_to(factor_b.T[None], (chips, width, cols_j))
    mine = lax.all_to_all(copies, "row", 0, 0, axis_index_groups=same_core)
    other = lax.ppermute(mine, "row", swap)
    block, parts = partial_gram(mine, other, own_gram(mine), n_col)
    parts = lax.all_to_all(parts, "col", 0, 0)
    terms, gram_c = mttkrp(core, tensor, block, factor_c)
    packed = lax.all_to_all(pack(parts, terms), "col", 0, 0)
    other = lax.ppermute(packed[:, : parts.shape[1]], "row", swap)
    own, change = first_half(packed, gram_c)
    solved, squares = solve(core, own, change, packed, other, gram_c)
    squares = squares + lax.ppermute(squares, "row", swap)
    same_core = [
        [(2 * chip + core) * n_col + c for chip in range(chips) for c in range(n_col)]
        for core in range(2)
    ]
    copies = jnp.broadcast_to(squares[None], (chips * n_col,) + squares.shape)
    squares = lax.all_to_all(copies, both, 0, 0, axis_index_groups=same_core)
    factor_a, col_scale = finish(squares, solved, rows_i * n_row)
    return (factor_a, col_scale[0])


def solution(mesh):
    return jax.shard_map(
        local,
        mesh=mesh,
        in_specs=(P(None, "row", "col"), P("col", "row"), P()),
        out_specs=(P(both, None), P()),
        check_vma=False,
    )
```

```python
import functools

import jax
import jax.numpy as jnp
from jax import lax
from jax.experimental import pallas as pl
from jax.experimental.pallas import tpu as pltpu
from jax.sharding import PartitionSpec as P

eps = 1e-06
high = lax.Precision.HIGHEST
f32 = jnp.float32
bf16 = jnp.bfloat16
limit = 16 * 1024 * 1024
wide = 52 * 1024 * 1024
beside = 10**10
pivots = 16
lanes = 128
frames = (4, 12, 16)
both = ("row", "col")
nt = (((1,), (1,)), ((), ()))


def gram_kernel(mine_ref, other_ref, block_ref, part_ref):
    mine = mine_ref[...].reshape(part_ref.shape[0] * part_ref.shape[1], block_ref.shape[1])
    block_ref[: mine.shape[0]] = mine
    block_ref[mine.shape[0] :] = other_ref[...].reshape(mine.shape)
    part = lax.dot_general(mine, block_ref[...], nt, precision=high, preferred_element_type=f32)
    part_ref[...] = part.reshape(part_ref.shape)


def partial_gram(mine, other, peers):
    count, width, cols_j = mine.shape
    ranks = 2 * count * width
    return pl.pallas_call(
        gram_kernel,
        out_shape=(
            jax.ShapeDtypeStruct((ranks, cols_j), f32),
            jax.ShapeDtypeStruct((peers, ranks // 2 // peers, ranks), f32),
        ),
        compiler_params=pltpu.CompilerParams(vmem_limit_bytes=limit),
        cost_estimate=pl.CostEstimate(
            flops=beside, bytes_accessed=8 * ranks * cols_j, transcendentals=0
        ),
        name="gram_part",
    )(mine, other)


def own_first(core, value):
    front, back = value[:, :lanes], value[:, lanes:]
    lane = lax.broadcasted_iota(jnp.int32, front.shape, 1)
    tiles = []
    for whose in (core, 1 - core):
        index = 32 * (lane // 16 % 4) + 16 * whose + lane % 16
        low, top = (jnp.take_along_axis(part, index, axis=1) for part in (front, back))
        tiles.append(jnp.where(lane < lanes // 2, low, top))
    return jnp.concatenate(tiles, axis=1)


def by_turns(core, value):
    own, other = value[:, :lanes], value[:, lanes:]
    lane = lax.broadcasted_iota(jnp.int32, own.shape, 1)
    tiles = []
    for t in range(2):
        index = 16 * (4 * t + lane // 32) + lane % 16
        ours, theirs = (jnp.take_along_axis(part, index, axis=1) for part in (own, other))
        tiles.append(jnp.where(lane // 16 % 2 == core, ours, theirs))
    return jnp.concatenate(tiles, axis=1)


def halves(value):
    top = value.astype(bf16)
    return top, (value - top.astype(f32)).astype(bf16)


def mttkrp_kernel(core_ref, slab_hbm, block_ref, c_ref, out_ref, gram_c_ref, slab_ref, arrived):
    pieces = []
    first = 0
    for part, count in enumerate(frames):
        here = pl.ds(first, count)
        copy = pltpu.make_async_copy(slab_hbm.at[here], slab_ref.at[here], arrived.at[part])
        pieces.append((copy, range(first, first + count)))
        first += count
    for copy, _ in pieces:
        copy.start()
    c = own_first(core_ref[0], c_ref[...])
    gram_c_ref[...] = lax.dot_general(
        c, c, (((0,), (0,)), ((), ())), precision=high, preferred_element_type=f32
    )
    top, low = halves(block_ref[...])
    weights = jnp.concatenate([top, low, top], axis=1)
    total = jnp.zeros(out_ref.shape, f32)
    for copy, here in pieces:
        copy.wait()
        for k in here:
            top, low = halves(slab_ref[k])
            product = lax.dot_general(
                jnp.concatenate([top, top, low], axis=1), weights, nt, preferred_element_type=f32
            )
            total += product * c[k : k + 1]
    out_ref[...] = total


def mttkrp(core, slab, block, factor_c):
    depth, rows_i, cols_j = slab.shape
    ranks = block.shape[0]
    return pl.pallas_call(
        mttkrp_kernel,
        out_shape=(
            jax.ShapeDtypeStruct((rows_i, ranks), f32),
            jax.ShapeDtypeStruct((ranks, ranks), f32),
        ),
        in_specs=[pl.BlockSpec(memory_space=pltpu.SMEM), pl.BlockSpec(memory_space=pl.ANY)]
        + [pl.BlockSpec(memory_space=pltpu.VMEM)] * 2,
        scratch_shapes=[
            pltpu.VMEM(slab.shape, f32),
            pltpu.SemaphoreType.DMA((len(frames),)),
        ],
        compiler_params=pltpu.CompilerParams(vmem_limit_bytes=wide),
        cost_estimate=pl.CostEstimate(
            flops=6 * depth * rows_i * cols_j * ranks,
            bytes_accessed=4 * depth * rows_i * cols_j,
            transcendentals=0,
        ),
        name="mttkrp",
    )(core, slab, block, factor_c)


def pack_kernel(parts_ref, terms_ref, out_ref):
    rows = parts_ref.shape[1]
    total = jnp.sum(parts_ref[...], axis=0)
    out_ref[:, :rows] = jnp.broadcast_to(total[None], parts_ref.shape)
    out_ref[:, rows:] = terms_ref[...].reshape(out_ref[:, rows:].shape)


def pack(parts, terms):
    peers, rows, ranks = parts.shape
    return pl.pallas_call(
        pack_kernel,
        out_shape=jax.ShapeDtypeStruct((peers, rows + terms.shape[0] // peers, ranks), f32),
        compiler_params=pltpu.CompilerParams(vmem_limit_bytes=limit),
        name="pack",
    )(parts, terms)


def split(value):
    top = value.astype(bf16)
    rest = value - top.astype(f32)
    middle = rest.astype(bf16)
    return top, middle, (rest - middle.astype(f32)).astype(bf16)


def left_parts(value):
    top, middle, low = split(value)
    return jnp.concatenate([top, top, middle, top, middle, low], axis=0)


def right_parts(value):
    top, middle, low = split(value)
    return jnp.concatenate([top, middle, top, low, middle, top], axis=0)


def spread(block, offset):
    return [
        jnp.broadcast_to(block[:, offset + q : offset + q + 1], block.shape) for q in range(pivots)
    ]


def over_rows(tile, q):
    return jnp.broadcast_to(tile[q : q + 1], tile.shape)


def eliminate(tiles, tile, offset):
    shape = tiles[0].shape
    row = lax.broadcasted_iota(jnp.int32, shape, 0)
    lane = lax.broadcasted_iota(jnp.int32, shape, 1) - offset
    cols = spread(tiles[tile], offset)
    tiles = list(tiles)
    unit = jnp.where(lane == row, 1.0, 0.0)
    tiles[tile] = jnp.where((lane >= 0) & (lane < pivots), unit, tiles[tile])
    scale = jnp.ones(shape, f32)
    pivot = over_rows(cols[0], 0)
    for q in range(pivots):
        here = row == q
        inverse = 1.0 / pivot
        near = range(q + 1, min(q + 1 + 1, pivots))
        masked = jnp.where(here, 0.0, cols[q])
        change = [masked * over_rows(cols[p], q) for p in near]
        if q + 1 < pivots:
            pivot = over_rows(cols[q + 1], q + 1) - over_rows(change[0], q + 1) * inverse
        factor = masked * inverse
        scale = jnp.where(here, inverse, scale)
        for p, term in zip(near, change):
            cols[p] = cols[p] - term * inverse
        for p in range(q + 1 + 1, pivots):
            cols[p] = cols[p] - factor * over_rows(cols[p], q)
        tiles = [part - factor * over_rows(part, q) for part in tiles]
    return [part * scale for part in tiles]


def invert(gram_ref, begin, end):
    size, ranks = gram_ref.shape
    starts = range(0, ranks, lanes)
    lane = lax.broadcasted_iota(jnp.int32, (pivots, lanes), 1)
    for k0 in range(begin, end, pivots):
        k1 = k0 + pivots
        k2 = min(k1 + pivots, size)
        tile, offset = k0 // lanes, k0 % lanes

        def without_block(rows, t):
            here = lax.broadcasted_iota(jnp.int32, rows.shape, 1) - offset
            return jnp.where((here >= 0) & (here < pivots), 0.0, rows) if t == tile else rows

        head = [gram_ref[k0:k1, t : t + lanes] for t in starts]
        signed = [jnp.where(lane < k0 - t, -part, part) for part, t in zip(head, starts)]
        left = left_parts(jnp.concatenate(signed[: size // lanes], axis=1))
        if k2 > k1:
            ahead = spread(gram_ref[k1:k2, tile * lanes : (tile + 1) * lanes], offset)
        done = eliminate(head, tile, offset)
        for t, part in enumerate(done):
            here = slice(t * lanes, (t + 1) * lanes)
            if k2 > k1:
                sums = [ahead[q] * over_rows(part, q) for q in range(4)]
                for q in range(4, pivots):
                    sums[q % 4] = sums[q % 4] + ahead[q] * over_rows(part, q)
                change = (sums[0] + sums[1]) + (sums[2] + sums[3])
                gram_ref[k1:k2, here] = without_block(gram_ref[k1:k2, here], t) - change
        update = lax.dot_general(
            left, right_parts(jnp.concatenate(done, axis=1)), (((0,), (0,)), ((), ())),
            preferred_element_type=f32,
        )
        for t, part in enumerate(done):
            here = slice(t * lanes, (t + 1) * lanes)
            for first, last in ((k2, size), (0, k0)):
                if first < last:
                    rows = without_block(gram_ref[first:last, here], t)
                    gram_ref[first:last, here] = rows - update[first:last, here]
            gram_ref[k0:k1, here] = part


def first_kernel(packed_ref, gram_c_ref, own_ref, change_ref):
    half, ranks = own_ref.shape
    rows = half // packed_ref.shape[0]
    own = packed_ref[:, :rows].reshape(half, ranks) * gram_c_ref[:half]
    own_ref[...] = own
    left = left_parts(own[:, half:])
    invert(own_ref, 0, half)
    change_ref[...] = lax.dot_general(
        left, right_parts(own_ref[...]), (((0,), (0,)), ((), ())), preferred_element_type=f32
    )


def first_half(packed, gram_c):
    half = jax.ShapeDtypeStruct((gram_c.shape[0] // 2, gram_c.shape[1]), f32)
    return pl.pallas_call(
        first_kernel,
        out_shape=(half, half),
        compiler_params=pltpu.CompilerParams(vmem_limit_bytes=limit),
        cost_estimate=pl.CostEstimate(
            flops=beside, bytes_accessed=packed.size * 4, transcendentals=0
        ),
        name="first_half",
    )(packed, gram_c)


def solve_kernel(
    core_ref, own_ref, change_ref, packed_ref, other_ref, gram_c_ref, solved_ref, squares_ref, gram_ref
):
    half, ranks = own_ref.shape
    rows = other_ref.shape[1]
    gram_ref[:half] = own_ref[...]
    other = other_ref[...].reshape(half, ranks)[:, :half] * gram_c_ref[half:, half:]
    gram_ref[half:, :half] = -change_ref[:, :half]
    gram_ref[half:, half:] = other - change_ref[:, half:]
    invert(gram_ref, half, ranks)
    mine = jnp.sum(packed_ref[:, rows:], axis=0)
    solved = jnp.dot(mine, gram_ref[...], precision=high, preferred_element_type=f32)
    solved = by_turns(core_ref[0], solved)
    solved_ref[...] = solved
    squares_ref[...] = jnp.sum(solved * solved, axis=0, keepdims=True)


def solve(core, own, change, packed, other, gram_c):
    peers, rows, ranks = other.shape
    return pl.pallas_call(
        solve_kernel,
        out_shape=(
            jax.ShapeDtypeStruct((packed.shape[1] - rows, ranks), f32),
            jax.ShapeDtypeStruct((1, ranks), f32),
        ),
        in_specs=[pl.BlockSpec(memory_space=pltpu.SMEM)]
        + [pl.BlockSpec(memory_space=pltpu.VMEM)] * 5,
        scratch_shapes=[pltpu.VMEM((ranks, ranks), f32)],
        compiler_params=pltpu.CompilerParams(vmem_limit_bytes=limit),
        name="solve",
    )(core, own, change, packed, other, gram_c)


def finish_kernel(count, squares_ref, solved_ref, factor_ref, scale_ref):
    squares = jnp.sum(squares_ref[...], axis=0)
    scale = jnp.sqrt(squares / count + eps)
    scale_ref[...] = scale
    factor_ref[...] = solved_ref[...] / scale


def finish(squares, solved, count):
    return pl.pallas_call(
        functools.partial(finish_kernel, count),
        out_shape=(
            jax.ShapeDtypeStruct(solved.shape, f32),
            jax.ShapeDtypeStruct((1, solved.shape[1]), f32),
        ),
        compiler_params=pltpu.CompilerParams(vmem_limit_bytes=limit),
        name="finish",
    )(squares, solved)


def local(tensor, factor_b, factor_c):
    depth, rows_i, cols_j = tensor.shape
    n_row, n_col = lax.axis_size("row"), lax.axis_size("col")
    core = (lax.axis_index("row") % 2).astype(jnp.int32)[None]
    chips = n_row // 2
    same_core = [[2 * chip + core for chip in range(chips)] for core in range(2)]
    swap = [(i, i ^ 1) for i in range(n_row)]
    width = factor_b.shape[1]

    copies = jnp.broadcast_to(factor_b.T[None], (chips, width, cols_j))
    mine = lax.all_to_all(copies, "row", 0, 0, axis_index_groups=same_core)
    other = lax.ppermute(mine, "row", swap)
    block, parts = partial_gram(mine, other, n_col)
    parts = lax.all_to_all(parts, "col", 0, 0)
    terms, gram_c = mttkrp(core, tensor, block, factor_c)
    packed = lax.all_to_all(pack(parts, terms), "col", 0, 0)
    other = lax.ppermute(packed[:, : parts.shape[1]], "row", swap)
    own, change = first_half(packed, gram_c)
    solved, squares = solve(core, own, change, packed, other, gram_c)
    beside_x = [(i, i ^ 1) for i in range(n_col)]
    across = [((i * n_col) + j, (i ^ 1) * n_col + (j ^ 1)) for i in range(n_row) for j in range(n_col)]
    chip = squares + lax.ppermute(squares, "row", swap)
    neighbour = lax.ppermute(squares, "col", beside_x) + lax.ppermute(squares, both, across)
    squares = chip + neighbour
    group = [
        [
            (2 * pair + which) * n_col + c
            for pair in range(chips)
            for c in range(n_col)
            if c % 4 in ends
        ]
        for which in range(2)
        for ends in ((0, 3), (1, 2))
    ]
    copies = jnp.broadcast_to(squares[None], (len(group[0]),) + squares.shape)
    squares = lax.all_to_all(copies, both, 0, 0, axis_index_groups=group)
    factor_a, col_scale = finish(squares, solved, rows_i * n_row)
    return (factor_a, col_scale[0])


def solution(mesh):
    return jax.shard_map(
        local,
        mesh=mesh,
        in_specs=(P(None, "row", "col"), P("col", "row"), P()),
        out_specs=(P(both, None), P()),
        check_vma=False,
    )
```

```python
import functools

import jax
import jax.numpy as jnp
from jax import lax
from jax.experimental import pallas as pl
from jax.experimental.pallas import tpu as pltpu
from jax.sharding import PartitionSpec as P

eps = 1e-06
high = lax.Precision.HIGHEST
f32 = jnp.float32
bf16 = jnp.bfloat16
limit = 16 * 1024 * 1024
wide = 52 * 1024 * 1024
beside = 10**10
pivots = 16
lanes = 128
frames = (4, 12, 16)
both = ("row", "col")
nt = (((1,), (1,)), ((), ()))


def gram_kernel(mine_ref, other_ref, block_ref, part_ref):
    mine = mine_ref[...].reshape(part_ref.shape[0] * part_ref.shape[1], block_ref.shape[1])
    block_ref[: mine.shape[0]] = mine
    block_ref[mine.shape[0] :] = other_ref[...].reshape(mine.shape)
    part = lax.dot_general(
        left_parts(mine, 1), right_parts(block_ref[...], 1), nt, preferred_element_type=f32
    )
    part_ref[...] = part.reshape(part_ref.shape)


def partial_gram(mine, other, peers):
    count, width, cols_j = mine.shape
    ranks = 2 * count * width
    return pl.pallas_call(
        gram_kernel,
        out_shape=(
            jax.ShapeDtypeStruct((ranks, cols_j), f32),
            jax.ShapeDtypeStruct((peers, ranks // 2 // peers, ranks), f32),
        ),
        compiler_params=pltpu.CompilerParams(vmem_limit_bytes=limit),
        cost_estimate=pl.CostEstimate(
            flops=beside, bytes_accessed=8 * ranks * cols_j, transcendentals=0
        ),
        name="gram_part",
    )(mine, other)


def own_first(core, value):
    front, back = value[:, :lanes], value[:, lanes:]
    lane = lax.broadcasted_iota(jnp.int32, front.shape, 1)
    tiles = []
    for whose in (core, 1 - core):
        index = 32 * (lane // 16 % 4) + 16 * whose + lane % 16
        low, top = (jnp.take_along_axis(part, index, axis=1) for part in (front, back))
        tiles.append(jnp.where(lane < lanes // 2, low, top))
    return jnp.concatenate(tiles, axis=1)


def by_turns(core, value):
    own, other = value[:, :lanes], value[:, lanes:]
    lane = lax.broadcasted_iota(jnp.int32, own.shape, 1)
    tiles = []
    for t in range(2):
        index = 16 * (4 * t + lane // 32) + lane % 16
        ours, theirs = (jnp.take_along_axis(part, index, axis=1) for part in (own, other))
        tiles.append(jnp.where(lane // 16 % 2 == core, ours, theirs))
    return jnp.concatenate(tiles, axis=1)


def halves(value):
    top = value.astype(bf16)
    return top, (value - top.astype(f32)).astype(bf16)


def mttkrp_kernel(core_ref, slab_hbm, block_ref, c_ref, out_ref, gram_c_ref, slab_ref, arrived):
    pieces = []
    first = 0
    for part, count in enumerate(frames):
        here = pl.ds(first, count)
        copy = pltpu.make_async_copy(slab_hbm.at[here], slab_ref.at[here], arrived.at[part])
        pieces.append((copy, range(first, first + count)))
        first += count
    for copy, _ in pieces:
        copy.start()
    c = own_first(core_ref[0], c_ref[...])
    gram_c_ref[...] = lax.dot_general(
        c, c, (((0,), (0,)), ((), ())), precision=high, preferred_element_type=f32
    )
    top, low = halves(block_ref[...])
    weights = jnp.concatenate([top, low, top], axis=1)
    total = jnp.zeros(out_ref.shape, f32)
    for copy, here in pieces:
        copy.wait()
        for k in here:
            top, low = halves(slab_ref[k])
            product = lax.dot_general(
                jnp.concatenate([top, top, low], axis=1), weights, nt, preferred_element_type=f32
            )
            total += product * c[k : k + 1]
    out_ref[...] = total


def mttkrp(core, slab, block, factor_c):
    depth, rows_i, cols_j = slab.shape
    ranks = block.shape[0]
    return pl.pallas_call(
        mttkrp_kernel,
        out_shape=(
            jax.ShapeDtypeStruct((rows_i, ranks), f32),
            jax.ShapeDtypeStruct((ranks, ranks), f32),
        ),
        in_specs=[pl.BlockSpec(memory_space=pltpu.SMEM), pl.BlockSpec(memory_space=pl.ANY)]
        + [pl.BlockSpec(memory_space=pltpu.VMEM)] * 2,
        scratch_shapes=[
            pltpu.VMEM(slab.shape, f32),
            pltpu.SemaphoreType.DMA((len(frames),)),
        ],
        compiler_params=pltpu.CompilerParams(vmem_limit_bytes=wide),
        cost_estimate=pl.CostEstimate(
            flops=6 * depth * rows_i * cols_j * ranks,
            bytes_accessed=4 * depth * rows_i * cols_j,
            transcendentals=0,
        ),
        name="mttkrp",
    )(core, slab, block, factor_c)


def pack_kernel(parts_ref, terms_ref, out_ref):
    rows = parts_ref.shape[1]
    total = jnp.sum(parts_ref[...], axis=0)
    out_ref[:, :rows] = jnp.broadcast_to(total[None], parts_ref.shape)
    out_ref[:, rows:] = terms_ref[...].reshape(out_ref[:, rows:].shape)


def pack(parts, terms):
    peers, rows, ranks = parts.shape
    return pl.pallas_call(
        pack_kernel,
        out_shape=jax.ShapeDtypeStruct((peers, rows + terms.shape[0] // peers, ranks), f32),
        compiler_params=pltpu.CompilerParams(vmem_limit_bytes=limit),
        name="pack",
    )(parts, terms)


def split(value):
    top = value.astype(bf16)
    rest = value - top.astype(f32)
    middle = rest.astype(bf16)
    return top, middle, (rest - middle.astype(f32)).astype(bf16)


def left_parts(value, axis=0):
    top, middle, low = split(value)
    return jnp.concatenate([top, top, middle, top, middle, low], axis=axis)


def right_parts(value, axis=0):
    top, middle, low = split(value)
    return jnp.concatenate([top, middle, top, low, middle, top], axis=axis)


def spread(block, offset):
    return [
        jnp.broadcast_to(block[:, offset + q : offset + q + 1], block.shape) for q in range(pivots)
    ]


def over_rows(tile, q):
    return jnp.broadcast_to(tile[q : q + 1], tile.shape)


def eliminate(tiles, tile, offset):
    shape = tiles[0].shape
    row = lax.broadcasted_iota(jnp.int32, shape, 0)
    lane = lax.broadcasted_iota(jnp.int32, shape, 1) - offset
    cols = spread(tiles[tile], offset)
    tiles = list(tiles)
    unit = jnp.where(lane == row, 1.0, 0.0)
    tiles[tile] = jnp.where((lane >= 0) & (lane < pivots), unit, tiles[tile])
    scale = jnp.ones(shape, f32)
    for q in range(pivots):
        here = row == q
        if q + 1 < pivots:
            change = jnp.where(here, 0.0, cols[q] * over_rows(cols[q + 1], q))
        inverse = jnp.broadcast_to(1.0 / cols[q][q : q + 1], shape)
        factor = jnp.where(here, 0.0, cols[q] * inverse)
        scale = jnp.where(here, inverse, scale)
        if q + 1 < pivots:
            cols[q + 1] = cols[q + 1] - change * inverse
        for p in range(q + 2, pivots):
            cols[p] = cols[p] - factor * over_rows(cols[p], q)
        tiles = [part - factor * over_rows(part, q) for part in tiles]
    return [part * scale for part in tiles]


def invert(gram_ref, begin, end):
    size, ranks = gram_ref.shape
    starts = range(0, ranks, lanes)
    lane = lax.broadcasted_iota(jnp.int32, (pivots, lanes), 1)
    for k0 in range(begin, end, pivots):
        k1 = k0 + pivots
        k2 = min(k1 + pivots, size)
        tile, offset = k0 // lanes, k0 % lanes

        def without_block(rows, t):
            here = lax.broadcasted_iota(jnp.int32, rows.shape, 1) - offset
            return jnp.where((here >= 0) & (here < pivots), 0.0, rows) if t == tile else rows

        head = [gram_ref[k0:k1, t : t + lanes] for t in starts]
        signed = [jnp.where(lane < k0 - t, -part, part) for part, t in zip(head, starts)]
        left = left_parts(jnp.concatenate(signed[: size // lanes], axis=1))
        if k2 > k1:
            ahead = spread(gram_ref[k1:k2, tile * lanes : (tile + 1) * lanes], offset)
        done = eliminate(head, tile, offset)
        for t, part in enumerate(done):
            here = slice(t * lanes, (t + 1) * lanes)
            if k2 > k1:
                sums = [ahead[q] * over_rows(part, q) for q in range(4)]
                for q in range(4, pivots):
                    sums[q % 4] = sums[q % 4] + ahead[q] * over_rows(part, q)
                change = (sums[0] + sums[1]) + (sums[2] + sums[3])
                gram_ref[k1:k2, here] = without_block(gram_ref[k1:k2, here], t) - change
        update = lax.dot_general(
            left, right_parts(jnp.concatenate(done, axis=1)), (((0,), (0,)), ((), ())),
            preferred_element_type=f32,
        )
        for t, part in enumerate(done):
            here = slice(t * lanes, (t + 1) * lanes)
            for first, last in ((k2, size), (0, k0)):
                if first < last:
                    rows = without_block(gram_ref[first:last, here], t)
                    gram_ref[first:last, here] = rows - update[first:last, here]
            gram_ref[k0:k1, here] = part


def first_kernel(packed_ref, gram_c_ref, own_ref, change_ref):
    half, ranks = own_ref.shape
    rows = half // packed_ref.shape[0]
    own = packed_ref[:, :rows].reshape(half, ranks) * gram_c_ref[:half]
    own_ref[...] = own
    left = left_parts(own[:, half:])
    invert(own_ref, 0, half)
    change_ref[...] = lax.dot_general(
        left, right_parts(own_ref[...]), (((0,), (0,)), ((), ())), preferred_element_type=f32
    )


def first_half(packed, gram_c):
    half = jax.ShapeDtypeStruct((gram_c.shape[0] // 2, gram_c.shape[1]), f32)
    return pl.pallas_call(
        first_kernel,
        out_shape=(half, half),
        compiler_params=pltpu.CompilerParams(vmem_limit_bytes=limit),
        cost_estimate=pl.CostEstimate(
            flops=beside, bytes_accessed=packed.size * 4, transcendentals=0
        ),
        name="first_half",
    )(packed, gram_c)


def solve_kernel(
    core_ref, own_ref, change_ref, packed_ref, other_ref, gram_c_ref, solved_ref, squares_ref, gram_ref
):
    half, ranks = own_ref.shape
    rows = other_ref.shape[1]
    gram_ref[:half] = own_ref[...]
    other = other_ref[...].reshape(half, ranks)[:, :half] * gram_c_ref[half:, half:]
    gram_ref[half:, :half] = -change_ref[:, :half]
    gram_ref[half:, half:] = other - change_ref[:, half:]
    invert(gram_ref, half, ranks)
    mine = jnp.sum(packed_ref[:, rows:], axis=0)
    solved = jnp.dot(
        left_parts(mine, 1), right_parts(gram_ref[...]), preferred_element_type=f32
    )
    solved = by_turns(core_ref[0], solved)
    solved_ref[...] = solved
    squares_ref[...] = jnp.sum(solved * solved, axis=0, keepdims=True)


def solve(core, own, change, packed, other, gram_c):
    peers, rows, ranks = other.shape
    return pl.pallas_call(
        solve_kernel,
        out_shape=(
            jax.ShapeDtypeStruct((packed.shape[1] - rows, ranks), f32),
            jax.ShapeDtypeStruct((1, ranks), f32),
        ),
        in_specs=[pl.BlockSpec(memory_space=pltpu.SMEM)]
        + [pl.BlockSpec(memory_space=pltpu.VMEM)] * 5,
        scratch_shapes=[pltpu.VMEM((ranks, ranks), f32)],
        compiler_params=pltpu.CompilerParams(vmem_limit_bytes=limit),
        name="solve",
    )(core, own, change, packed, other, gram_c)


def finish_kernel(count, squares_ref, solved_ref, factor_ref, scale_ref):
    squares = jnp.sum(squares_ref[...], axis=0)
    scale = jnp.sqrt(squares / count + eps)
    scale_ref[...] = scale
    factor_ref[...] = solved_ref[...] / scale


def finish(squares, solved, count):
    return pl.pallas_call(
        functools.partial(finish_kernel, count),
        out_shape=(
            jax.ShapeDtypeStruct(solved.shape, f32),
            jax.ShapeDtypeStruct((1, solved.shape[1]), f32),
        ),
        compiler_params=pltpu.CompilerParams(vmem_limit_bytes=limit),
        name="finish",
    )(squares, solved)


def local(tensor, factor_b, factor_c):
    depth, rows_i, cols_j = tensor.shape
    n_row, n_col = lax.axis_size("row"), lax.axis_size("col")
    core = (lax.axis_index("row") % 2).astype(jnp.int32)[None]
    chips = n_row // 2
    same_core = [[2 * chip + core for chip in range(chips)] for core in range(2)]
    swap = [(i, i ^ 1) for i in range(n_row)]
    width = factor_b.shape[1]

    copies = jnp.broadcast_to(factor_b.T[None], (chips, width, cols_j))
    mine = lax.all_to_all(copies, "row", 0, 0, axis_index_groups=same_core)
    other = lax.ppermute(mine, "row", swap)
    block, parts = partial_gram(mine, other, n_col)
    parts = lax.all_to_all(parts, "col", 0, 0)
    terms, gram_c = mttkrp(core, tensor, block, factor_c)
    packed = lax.all_to_all(pack(parts, terms), "col", 0, 0)
    other = lax.ppermute(packed[:, : parts.shape[1]], "row", swap)
    own, change = first_half(packed, gram_c)
    solved, squares = solve(core, own, change, packed, other, gram_c)
    squares = squares + lax.ppermute(squares, "row", swap)
    same_core = [
        [(2 * chip + core) * n_col + c for chip in range(chips) for c in range(n_col)]
        for core in range(2)
    ]
    copies = jnp.broadcast_to(squares[None], (chips * n_col,) + squares.shape)
    squares = lax.all_to_all(copies, both, 0, 0, axis_index_groups=same_core)
    factor_a, col_scale = finish(squares, solved, rows_i * n_row)
    return (factor_a, col_scale[0])


def solution(mesh):
    return jax.shard_map(
        local,
        mesh=mesh,
        in_specs=(P(None, "row", "col"), P("col", "row"), P()),
        out_specs=(P(both, None), P()),
        check_vma=False,
    )
```

```python
import functools

import jax
import jax.numpy as jnp
from jax import lax
from jax.experimental import pallas as pl
from jax.experimental.pallas import tpu as pltpu
from jax.sharding import PartitionSpec as P

eps = 1e-06
high = lax.Precision.HIGHEST
f32 = jnp.float32
bf16 = jnp.bfloat16
limit = 16 * 1024 * 1024
wide = 52 * 1024 * 1024
beside = 10**10
pivots = 16
lanes = 128
frames = (4, 12, 16)
both = ("row", "col")
nt = (((1,), (1,)), ((), ()))


def rank_gram(left, right):
    return lax.dot_general(left, right, nt, precision=high, preferred_element_type=f32)


def own_kernel(mine_ref, own_ref):
    mine = mine_ref[...].reshape(own_ref.shape[0], mine_ref.shape[2])
    own_ref[...] = rank_gram(mine, mine)


def own_gram(mine):
    half = mine.shape[0] * mine.shape[1]
    return pl.pallas_call(
        own_kernel,
        out_shape=jax.ShapeDtypeStruct((half, half), f32),
        compiler_params=pltpu.CompilerParams(vmem_limit_bytes=limit),
        name="gram_own",
    )(mine)


def gram_kernel(mine_ref, other_ref, own_ref, block_ref, part_ref):
    half = own_ref.shape[0]
    mine = mine_ref[...].reshape(half, block_ref.shape[1])
    other = other_ref[...].reshape(mine.shape)
    block_ref[:half] = mine
    block_ref[half:] = other
    part_ref[:, :, :half] = own_ref[...].reshape(part_ref.shape[:2] + (half,))
    part_ref[:, :, half:] = rank_gram(mine, other).reshape(part_ref.shape[:2] + (half,))


def partial_gram(mine, other, own, peers):
    count, width, cols_j = mine.shape
    ranks = 2 * count * width
    return pl.pallas_call(
        gram_kernel,
        out_shape=(
            jax.ShapeDtypeStruct((ranks, cols_j), f32),
            jax.ShapeDtypeStruct((peers, ranks // 2 // peers, ranks), f32),
        ),
        compiler_params=pltpu.CompilerParams(vmem_limit_bytes=limit),
        cost_estimate=pl.CostEstimate(
            flops=beside, bytes_accessed=8 * ranks * cols_j, transcendentals=0
        ),
        name="gram_part",
    )(mine, other, own)


def own_first(core, value):
    front, back = value[:, :lanes], value[:, lanes:]
    lane = lax.broadcasted_iota(jnp.int32, front.shape, 1)
    tiles = []
    for whose in (core, 1 - core):
        index = 32 * (lane // 16 % 4) + 16 * whose + lane % 16
        low, top = (jnp.take_along_axis(part, index, axis=1) for part in (front, back))
        tiles.append(jnp.where(lane < lanes // 2, low, top))
    return jnp.concatenate(tiles, axis=1)


def by_turns(core, value):
    own, other = value[:, :lanes], value[:, lanes:]
    lane = lax.broadcasted_iota(jnp.int32, own.shape, 1)
    tiles = []
    for t in range(2):
        index = 16 * (4 * t + lane // 32) + lane % 16
        ours, theirs = (jnp.take_along_axis(part, index, axis=1) for part in (own, other))
        tiles.append(jnp.where(lane // 16 % 2 == core, ours, theirs))
    return jnp.concatenate(tiles, axis=1)


def halves(value):
    top = value.astype(bf16)
    return top, (value - top.astype(f32)).astype(bf16)


def mttkrp_kernel(core_ref, slab_hbm, block_ref, c_ref, out_ref, gram_c_ref, slab_ref, arrived):
    pieces = []
    first = 0
    for part, count in enumerate(frames):
        here = pl.ds(first, count)
        copy = pltpu.make_async_copy(slab_hbm.at[here], slab_ref.at[here], arrived.at[part])
        pieces.append((copy, range(first, first + count)))
        first += count
    for copy, _ in pieces:
        copy.start()
    c = own_first(core_ref[0], c_ref[...])
    gram_c_ref[...] = lax.dot_general(
        c, c, (((0,), (0,)), ((), ())), precision=high, preferred_element_type=f32
    )
    top, low = halves(block_ref[...])
    weights = jnp.concatenate([top, low, top], axis=1)
    total = jnp.zeros(out_ref.shape, f32)
    for copy, here in pieces:
        copy.wait()
        for k in here:
            top, low = halves(slab_ref[k])
            product = lax.dot_general(
                jnp.concatenate([top, top, low], axis=1), weights, nt, preferred_element_type=f32
            )
            total += product * c[k : k + 1]
    out_ref[...] = total


def mttkrp(core, slab, block, factor_c):
    depth, rows_i, cols_j = slab.shape
    ranks = block.shape[0]
    return pl.pallas_call(
        mttkrp_kernel,
        out_shape=(
            jax.ShapeDtypeStruct((rows_i, ranks), f32),
            jax.ShapeDtypeStruct((ranks, ranks), f32),
        ),
        in_specs=[pl.BlockSpec(memory_space=pltpu.SMEM), pl.BlockSpec(memory_space=pl.ANY)]
        + [pl.BlockSpec(memory_space=pltpu.VMEM)] * 2,
        scratch_shapes=[
            pltpu.VMEM(slab.shape, f32),
            pltpu.SemaphoreType.DMA((len(frames),)),
        ],
        compiler_params=pltpu.CompilerParams(vmem_limit_bytes=wide),
        cost_estimate=pl.CostEstimate(
            flops=6 * depth * rows_i * cols_j * ranks,
            bytes_accessed=4 * depth * rows_i * cols_j,
            transcendentals=0,
        ),
        name="mttkrp",
    )(core, slab, block, factor_c)


def pack_kernel(parts_ref, terms_ref, out_ref):
    rows = parts_ref.shape[1]
    total = jnp.sum(parts_ref[...], axis=0)
    out_ref[:, :rows] = jnp.broadcast_to(total[None], parts_ref.shape)
    out_ref[:, rows:] = terms_ref[...].reshape(out_ref[:, rows:].shape)


def pack(parts, terms):
    peers, rows, ranks = parts.shape
    return pl.pallas_call(
        pack_kernel,
        out_shape=jax.ShapeDtypeStruct((peers, rows + terms.shape[0] // peers, ranks), f32),
        compiler_params=pltpu.CompilerParams(vmem_limit_bytes=limit),
        name="pack",
    )(parts, terms)


def split(value):
    top = value.astype(bf16)
    rest = value - top.astype(f32)
    middle = rest.astype(bf16)
    return top, middle, (rest - middle.astype(f32)).astype(bf16)


def left_parts(value):
    top, middle, low = split(value)
    return jnp.concatenate([top, top, middle, top, middle, low], axis=0)


def right_parts(value):
    top, middle, low = split(value)
    return jnp.concatenate([top, middle, top, low, middle, top], axis=0)


def spread(block, offset):
    return [
        jnp.broadcast_to(block[:, offset + q : offset + q + 1], block.shape) for q in range(pivots)
    ]


def over_rows(tile, q):
    return jnp.broadcast_to(tile[q : q + 1], tile.shape)


def eliminate(tiles, tile, offset):
    shape = tiles[0].shape
    row = lax.broadcasted_iota(jnp.int32, shape, 0)
    lane = lax.broadcasted_iota(jnp.int32, shape, 1) - offset
    cols = spread(tiles[tile], offset)
    tiles = list(tiles)
    unit = jnp.where(lane == row, 1.0, 0.0)
    tiles[tile] = jnp.where((lane >= 0) & (lane < pivots), unit, tiles[tile])
    scale = jnp.ones(shape, f32)
    for q in range(pivots):
        here = row == q
        if q + 1 < pivots:
            change = jnp.where(here, 0.0, cols[q] * over_rows(cols[q + 1], q))
        inverse = jnp.broadcast_to(1.0 / cols[q][q : q + 1], shape)
        factor = jnp.where(here, 0.0, cols[q] * inverse)
        scale = jnp.where(here, inverse, scale)
        if q + 1 < pivots:
            cols[q + 1] = cols[q + 1] - change * inverse
        for p in range(q + 2, pivots):
            cols[p] = cols[p] - factor * over_rows(cols[p], q)
        tiles = [part - factor * over_rows(part, q) for part in tiles]
    return [part * scale for part in tiles]


def invert(gram_ref, begin, end):
    size, ranks = gram_ref.shape
    starts = range(0, ranks, lanes)
    lane = lax.broadcasted_iota(jnp.int32, (pivots, lanes), 1)
    for k0 in range(begin, end, pivots):
        k1 = k0 + pivots
        k2 = min(k1 + pivots, size)
        tile, offset = k0 // lanes, k0 % lanes

        def without_block(rows, t):
            here = lax.broadcasted_iota(jnp.int32, rows.shape, 1) - offset
            return jnp.where((here >= 0) & (here < pivots), 0.0, rows) if t == tile else rows

        head = [gram_ref[k0:k1, t : t + lanes] for t in starts]
        signed = [jnp.where(lane < k0 - t, -part, part) for part, t in zip(head, starts)]
        left = left_parts(jnp.concatenate(signed[: size // lanes], axis=1))
        if k2 > k1:
            ahead = spread(gram_ref[k1:k2, tile * lanes : (tile + 1) * lanes], offset)
        done = eliminate(head, tile, offset)
        for t, part in enumerate(done):
            here = slice(t * lanes, (t + 1) * lanes)
            if k2 > k1:
                sums = [ahead[q] * over_rows(part, q) for q in range(4)]
                for q in range(4, pivots):
                    sums[q % 4] = sums[q % 4] + ahead[q] * over_rows(part, q)
                change = (sums[0] + sums[1]) + (sums[2] + sums[3])
                gram_ref[k1:k2, here] = without_block(gram_ref[k1:k2, here], t) - change
        update = lax.dot_general(
            left, right_parts(jnp.concatenate(done, axis=1)), (((0,), (0,)), ((), ())),
            preferred_element_type=f32,
        )
        for t, part in enumerate(done):
            here = slice(t * lanes, (t + 1) * lanes)
            for first, last in ((k2, size), (0, k0)):
                if first < last:
                    rows = without_block(gram_ref[first:last, here], t)
                    gram_ref[first:last, here] = rows - update[first:last, here]
            gram_ref[k0:k1, here] = part


def first_kernel(packed_ref, gram_c_ref, own_ref, change_ref):
    half, ranks = own_ref.shape
    rows = half // packed_ref.shape[0]
    own = packed_ref[:, :rows].reshape(half, ranks) * gram_c_ref[:half]
    own_ref[...] = own
    left = left_parts(own[:, half:])
    invert(own_ref, 0, half)
    change_ref[...] = lax.dot_general(
        left, right_parts(own_ref[...]), (((0,), (0,)), ((), ())), preferred_element_type=f32
    )


def first_half(packed, gram_c):
    half = jax.ShapeDtypeStruct((gram_c.shape[0] // 2, gram_c.shape[1]), f32)
    return pl.pallas_call(
        first_kernel,
        out_shape=(half, half),
        compiler_params=pltpu.CompilerParams(vmem_limit_bytes=limit),
        cost_estimate=pl.CostEstimate(
            flops=beside, bytes_accessed=packed.size * 4, transcendentals=0
        ),
        name="first_half",
    )(packed, gram_c)


def solve_kernel(
    core_ref, own_ref, change_ref, packed_ref, other_ref, gram_c_ref, solved_ref, squares_ref, gram_ref
):
    half, ranks = own_ref.shape
    rows = other_ref.shape[1]
    gram_ref[:half] = own_ref[...]
    other = other_ref[...].reshape(half, ranks)[:, :half] * gram_c_ref[half:, half:]
    gram_ref[half:, :half] = -change_ref[:, :half]
    gram_ref[half:, half:] = other - change_ref[:, half:]
    invert(gram_ref, half, ranks)
    mine = jnp.sum(packed_ref[:, rows:], axis=0)
    solved = jnp.dot(mine, gram_ref[...], precision=high, preferred_element_type=f32)
    solved = by_turns(core_ref[0], solved)
    solved_ref[...] = solved
    squares_ref[...] = jnp.sum(solved * solved, axis=0, keepdims=True)


def solve(core, own, change, packed, other, gram_c):
    peers, rows, ranks = other.shape
    return pl.pallas_call(
        solve_kernel,
        out_shape=(
            jax.ShapeDtypeStruct((packed.shape[1] - rows, ranks), f32),
            jax.ShapeDtypeStruct((1, ranks), f32),
        ),
        in_specs=[pl.BlockSpec(memory_space=pltpu.SMEM)]
        + [pl.BlockSpec(memory_space=pltpu.VMEM)] * 5,
        scratch_shapes=[pltpu.VMEM((ranks, ranks), f32)],
        compiler_params=pltpu.CompilerParams(vmem_limit_bytes=limit),
        name="solve",
    )(core, own, change, packed, other, gram_c)


def finish_kernel(count, squares_ref, solved_ref, factor_ref, scale_ref):
    squares = jnp.sum(squares_ref[...], axis=0)
    scale = jnp.sqrt(squares / count + eps)
    scale_ref[...] = scale
    factor_ref[...] = solved_ref[...] / scale


def finish(squares, solved, count):
    return pl.pallas_call(
        functools.partial(finish_kernel, count),
        out_shape=(
            jax.ShapeDtypeStruct(solved.shape, f32),
            jax.ShapeDtypeStruct((1, solved.shape[1]), f32),
        ),
        compiler_params=pltpu.CompilerParams(vmem_limit_bytes=limit),
        name="finish",
    )(squares, solved)


def local(tensor, factor_b, factor_c):
    depth, rows_i, cols_j = tensor.shape
    n_row, n_col = lax.axis_size("row"), lax.axis_size("col")
    core = (lax.axis_index("row") % 2).astype(jnp.int32)[None]
    chips = n_row // 2
    same_core = [[2 * chip + core for chip in range(chips)] for core in range(2)]
    swap = [(i, i ^ 1) for i in range(n_row)]
    width = factor_b.shape[1]

    copies = jnp.broadcast_to(factor_b.T[None], (chips, width, cols_j))
    mine = lax.all_to_all(copies, "row", 0, 0, axis_index_groups=same_core)
    other = lax.ppermute(mine, "row", swap)
    block, parts = partial_gram(mine, other, own_gram(mine), n_col)
    parts = lax.all_to_all(parts, "col", 0, 0)
    terms, gram_c = mttkrp(core, tensor, block, factor_c)
    packed = lax.all_to_all(pack(parts, terms), "col", 0, 0)
    other = lax.ppermute(packed[:, : parts.shape[1]], "row", swap)
    own, change = first_half(packed, gram_c)
    solved, squares = solve(core, own, change, packed, other, gram_c)
    squares = squares + lax.ppermute(squares, "row", swap)
    same_core = [
        [(2 * chip + core) * n_col + c for chip in range(chips) for c in range(n_col)]
        for core in range(2)
    ]
    copies = jnp.broadcast_to(squares[None], (chips * n_col,) + squares.shape)
    squares = lax.all_to_all(copies, both, 0, 0, axis_index_groups=same_core)
    factor_a, col_scale = finish(squares, solved, rows_i * n_row)
    return (factor_a, col_scale[0])


def solution(mesh):
    return jax.shard_map(
        local,
        mesh=mesh,
        in_specs=(P(None, "row", "col"), P("col", "row"), P()),
        out_specs=(P(both, None), P()),
        check_vma=False,
    )
```

```python
import functools

import jax
import jax.numpy as jnp
from jax import lax
from jax.experimental import pallas as pl
from jax.experimental.pallas import tpu as pltpu
from jax.sharding import PartitionSpec as P

eps = 1e-06
high = lax.Precision.HIGHEST
f32 = jnp.float32
bf16 = jnp.bfloat16
limit = 16 * 1024 * 1024
wide = 52 * 1024 * 1024
beside = 10**10
pivots = 16
lanes = 128
frames = (4, 12, 16)
both = ("row", "col")
nt = (((1,), (1,)), ((), ()))


def rank_gram(left, right):
    return lax.dot_general(left, right, nt, precision=high, preferred_element_type=f32)


def own_kernel(mine_ref, own_ref):
    mine = mine_ref[...].reshape(own_ref.shape[0], mine_ref.shape[2])
    own_ref[...] = rank_gram(mine, mine)


def own_gram(mine):
    half = mine.shape[0] * mine.shape[1]
    return pl.pallas_call(
        own_kernel,
        out_shape=jax.ShapeDtypeStruct((half, half), f32),
        compiler_params=pltpu.CompilerParams(vmem_limit_bytes=limit),
        name="gram_own",
    )(mine)


def gram_kernel(mine_ref, other_ref, own_ref, block_ref, part_ref):
    half = own_ref.shape[0]
    mine = mine_ref[...].reshape(half, block_ref.shape[1])
    other = other_ref[...].reshape(mine.shape)
    block_ref[:half] = mine
    block_ref[half:] = other
    part_ref[:, :, :half] = own_ref[...].reshape(part_ref.shape[:2] + (half,))
    part_ref[:, :, half:] = rank_gram(mine, other).reshape(part_ref.shape[:2] + (half,))


def partial_gram(mine, other, own, peers):
    count, width, cols_j = mine.shape
    ranks = 2 * count * width
    return pl.pallas_call(
        gram_kernel,
        out_shape=(
            jax.ShapeDtypeStruct((ranks, cols_j), f32),
            jax.ShapeDtypeStruct((peers, ranks // 2 // peers, ranks), f32),
        ),
        compiler_params=pltpu.CompilerParams(vmem_limit_bytes=limit),
        cost_estimate=pl.CostEstimate(
            flops=beside, bytes_accessed=8 * ranks * cols_j, transcendentals=0
        ),
        name="gram_part",
    )(mine, other, own)


def own_first(core, value):
    front, back = value[:, :lanes], value[:, lanes:]
    lane = lax.broadcasted_iota(jnp.int32, front.shape, 1)
    tiles = []
    for whose in (core, 1 - core):
        index = 32 * (lane // 16 % 4) + 16 * whose + lane % 16
        low, top = (jnp.take_along_axis(part, index, axis=1) for part in (front, back))
        tiles.append(jnp.where(lane < lanes // 2, low, top))
    return jnp.concatenate(tiles, axis=1)


def by_turns(core, value):
    own, other = value[:, :lanes], value[:, lanes:]
    lane = lax.broadcasted_iota(jnp.int32, own.shape, 1)
    tiles = []
    for t in range(2):
        index = 16 * (4 * t + lane // 32) + lane % 16
        ours, theirs = (jnp.take_along_axis(part, index, axis=1) for part in (own, other))
        tiles.append(jnp.where(lane // 16 % 2 == core, ours, theirs))
    return jnp.concatenate(tiles, axis=1)


def halves(value):
    top = value.astype(bf16)
    return top, (value - top.astype(f32)).astype(bf16)


def mttkrp_kernel(core_ref, slab_hbm, block_ref, c_ref, out_ref, gram_c_ref, slab_ref, arrived):
    pieces = []
    first = 0
    for part, count in enumerate(frames):
        here = pl.ds(first, count)
        copy = pltpu.make_async_copy(slab_hbm.at[here], slab_ref.at[here], arrived.at[part])
        pieces.append((copy, range(first, first + count)))
        first += count
    for copy, _ in pieces:
        copy.start()
    c = own_first(core_ref[0], c_ref[...])
    gram_c_ref[...] = lax.dot_general(
        c, c, (((0,), (0,)), ((), ())), precision=high, preferred_element_type=f32
    )
    top, low = halves(block_ref[...])
    weights = jnp.concatenate([top, low, top], axis=1)
    total = jnp.zeros(out_ref.shape, f32)
    for copy, here in pieces:
        copy.wait()
        for k in here:
            top, low = halves(slab_ref[k])
            product = lax.dot_general(
                jnp.concatenate([top, top, low], axis=1), weights, nt, preferred_element_type=f32
            )
            total += product * c[k : k + 1]
    out_ref[...] = total


def mttkrp(core, slab, block, factor_c):
    depth, rows_i, cols_j = slab.shape
    ranks = block.shape[0]
    return pl.pallas_call(
        mttkrp_kernel,
        out_shape=(
            jax.ShapeDtypeStruct((rows_i, ranks), f32),
            jax.ShapeDtypeStruct((ranks, ranks), f32),
        ),
        in_specs=[pl.BlockSpec(memory_space=pltpu.SMEM), pl.BlockSpec(memory_space=pl.ANY)]
        + [pl.BlockSpec(memory_space=pltpu.VMEM)] * 2,
        scratch_shapes=[
            pltpu.VMEM(slab.shape, f32),
            pltpu.SemaphoreType.DMA((len(frames),)),
        ],
        compiler_params=pltpu.CompilerParams(vmem_limit_bytes=wide),
        cost_estimate=pl.CostEstimate(
            flops=6 * depth * rows_i * cols_j * ranks,
            bytes_accessed=4 * depth * rows_i * cols_j,
            transcendentals=0,
        ),
        name="mttkrp",
    )(core, slab, block, factor_c)


def pack_kernel(parts_ref, terms_ref, out_ref):
    rows = parts_ref.shape[1]
    total = jnp.sum(parts_ref[...], axis=0)
    out_ref[:, :rows] = jnp.broadcast_to(total[None], parts_ref.shape)
    out_ref[:, rows:] = terms_ref[...].reshape(out_ref[:, rows:].shape)


def pack(parts, terms):
    peers, rows, ranks = parts.shape
    return pl.pallas_call(
        pack_kernel,
        out_shape=jax.ShapeDtypeStruct((peers, rows + terms.shape[0] // peers, ranks), f32),
        compiler_params=pltpu.CompilerParams(vmem_limit_bytes=limit),
        name="pack",
    )(parts, terms)


def split(value):
    top = value.astype(bf16)
    rest = value - top.astype(f32)
    middle = rest.astype(bf16)
    return top, middle, (rest - middle.astype(f32)).astype(bf16)


def left_parts(value):
    top, middle, low = split(value)
    return jnp.concatenate([top, top, middle, top, middle, low], axis=0)


def right_parts(value):
    top, middle, low = split(value)
    return jnp.concatenate([top, middle, top, low, middle, top], axis=0)


def spread(block, offset):
    return [
        jnp.broadcast_to(block[:, offset + q : offset + q + 1], block.shape) for q in range(pivots)
    ]


def over_rows(tile, q):
    return jnp.broadcast_to(tile[q : q + 1], tile.shape)


def eliminate(tiles, tile, offset):
    shape = tiles[0].shape
    row = lax.broadcasted_iota(jnp.int32, shape, 0)
    lane = lax.broadcasted_iota(jnp.int32, shape, 1) - offset
    cols = spread(tiles[tile], offset)
    tiles = list(tiles)
    unit = jnp.where(lane == row, 1.0, 0.0)
    tiles[tile] = jnp.where((lane >= 0) & (lane < pivots), unit, tiles[tile])
    scale = jnp.ones(shape, f32)
    for q in range(pivots):
        here = row == q
        if q + 1 < pivots:
            change = jnp.where(here, 0.0, cols[q] * over_rows(cols[q + 1], q))
        inverse = jnp.broadcast_to(1.0 / cols[q][q : q + 1], shape)
        factor = jnp.where(here, 0.0, cols[q] * inverse)
        scale = jnp.where(here, inverse, scale)
        if q + 1 < pivots:
            cols[q + 1] = cols[q + 1] - change * inverse
        for p in range(q + 2, pivots):
            cols[p] = cols[p] - factor * over_rows(cols[p], q)
        tiles = [part - factor * over_rows(part, q) for part in tiles]
    return [part * scale for part in tiles]


def invert(gram_ref, begin, end):
    size, ranks = gram_ref.shape
    starts = range(0, ranks, lanes)
    lane = lax.broadcasted_iota(jnp.int32, (pivots, lanes), 1)
    for k0 in range(begin, end, pivots):
        k1 = k0 + pivots
        k2 = min(k1 + pivots, size)
        tile, offset = k0 // lanes, k0 % lanes

        def without_block(rows, t):
            here = lax.broadcasted_iota(jnp.int32, rows.shape, 1) - offset
            return jnp.where((here >= 0) & (here < pivots), 0.0, rows) if t == tile else rows

        head = [gram_ref[k0:k1, t : t + lanes] for t in starts]
        signed = [jnp.where(lane < k0 - t, -part, part) for part, t in zip(head, starts)]
        left = left_parts(jnp.concatenate(signed[: size // lanes], axis=1))
        if k2 > k1:
            ahead = spread(gram_ref[k1:k2, tile * lanes : (tile + 1) * lanes], offset)
        done = eliminate(head, tile, offset)
        for t, part in enumerate(done):
            here = slice(t * lanes, (t + 1) * lanes)
            if k2 > k1:
                sums = [ahead[q] * over_rows(part, q) for q in range(4)]
                for q in range(4, pivots):
                    sums[q % 4] = sums[q % 4] + ahead[q] * over_rows(part, q)
                change = (sums[0] + sums[1]) + (sums[2] + sums[3])
                gram_ref[k1:k2, here] = without_block(gram_ref[k1:k2, here], t) - change
        update = lax.dot_general(
            left, right_parts(jnp.concatenate(done, axis=1)), (((0,), (0,)), ((), ())),
            preferred_element_type=f32,
        )
        for t, part in enumerate(done):
            here = slice(t * lanes, (t + 1) * lanes)
            for first, last in ((k2, size), (0, k0)):
                if first < last:
                    rows = without_block(gram_ref[first:last, here], t)
                    gram_ref[first:last, here] = rows - update[first:last, here]
            gram_ref[k0:k1, here] = part


def first_kernel(packed_ref, gram_c_ref, own_ref, change_ref):
    half, ranks = own_ref.shape
    rows = half // packed_ref.shape[0]
    own = packed_ref[:, :rows].reshape(half, ranks) * gram_c_ref[:half]
    own_ref[...] = own
    left = left_parts(own[:, half:])
    invert(own_ref, 0, half)
    change_ref[...] = lax.dot_general(
        left, right_parts(own_ref[...]), (((0,), (0,)), ((), ())), preferred_element_type=f32
    )


def first_half(packed, gram_c):
    half = jax.ShapeDtypeStruct((gram_c.shape[0] // 2, gram_c.shape[1]), f32)
    return pl.pallas_call(
        first_kernel,
        out_shape=(half, half),
        compiler_params=pltpu.CompilerParams(vmem_limit_bytes=limit),
        cost_estimate=pl.CostEstimate(
            flops=beside, bytes_accessed=packed.size * 4, transcendentals=0
        ),
        name="first_half",
    )(packed, gram_c)


def solve_kernel(
    core_ref, own_ref, change_ref, packed_ref, other_ref, gram_c_ref, solved_ref, squares_ref, gram_ref
):
    half, ranks = own_ref.shape
    rows = other_ref.shape[1]
    gram_ref[:half] = own_ref[...]
    other = other_ref[...].reshape(half, ranks)[:, :half] * gram_c_ref[half:, half:]
    gram_ref[half:, :half] = -change_ref[:, :half]
    gram_ref[half:, half:] = other - change_ref[:, half:]
    invert(gram_ref, half, ranks)
    mine = jnp.sum(packed_ref[:, rows:], axis=0)
    solved = jnp.dot(mine, gram_ref[...], precision=high, preferred_element_type=f32)
    solved = by_turns(core_ref[0], solved)
    solved_ref[...] = solved
    squares_ref[...] = jnp.sum(solved * solved, axis=0, keepdims=True)


def solve(core, own, change, packed, other, gram_c):
    peers, rows, ranks = other.shape
    return pl.pallas_call(
        solve_kernel,
        out_shape=(
            jax.ShapeDtypeStruct((packed.shape[1] - rows, ranks), f32),
            jax.ShapeDtypeStruct((1, ranks), f32),
        ),
        in_specs=[pl.BlockSpec(memory_space=pltpu.SMEM)]
        + [pl.BlockSpec(memory_space=pltpu.VMEM)] * 5,
        scratch_shapes=[pltpu.VMEM((ranks, ranks), f32)],
        compiler_params=pltpu.CompilerParams(vmem_limit_bytes=limit),
        name="solve",
    )(core, own, change, packed, other, gram_c)


def finish_kernel(count, squares_ref, solved_ref, factor_ref, scale_ref):
    squares = jnp.sum(squares_ref[...], axis=0)
    scale = jnp.sqrt(squares / count + eps)
    scale_ref[...] = scale
    factor_ref[...] = solved_ref[...] / scale


def finish(squares, solved, count):
    return pl.pallas_call(
        functools.partial(finish_kernel, count),
        out_shape=(
            jax.ShapeDtypeStruct(solved.shape, f32),
            jax.ShapeDtypeStruct((1, solved.shape[1]), f32),
        ),
        compiler_params=pltpu.CompilerParams(vmem_limit_bytes=limit),
        name="finish",
    )(squares, solved)


def local(tensor, factor_b, factor_c):
    depth, rows_i, cols_j = tensor.shape
    n_row, n_col = lax.axis_size("row"), lax.axis_size("col")
    core = (lax.axis_index("row") % 2).astype(jnp.int32)[None]
    chips = n_row // 2
    same_core = [[2 * chip + core for chip in range(chips)] for core in range(2)]
    swap = [(i, i ^ 1) for i in range(n_row)]
    width = factor_b.shape[1]

    copies = jnp.broadcast_to(factor_b.T[None], (chips, width, cols_j))
    mine = lax.all_to_all(copies, "row", 0, 0, axis_index_groups=same_core)
    other = lax.ppermute(mine, "row", swap)
    block, parts = partial_gram(mine, other, own_gram(mine), n_col)
    parts = lax.all_to_all(parts, "col", 0, 0)
    terms, gram_c = mttkrp(core, tensor, block, factor_c)
    packed = lax.all_to_all(pack(parts, terms), "col", 0, 0)
    other = lax.ppermute(packed[:, : parts.shape[1]], "row", swap)
    own, change = first_half(packed, gram_c)
    solved, squares = solve(core, own, change, packed, other, gram_c)
    beside_x = [(i, i ^ 1) for i in range(n_col)]
    across = [((i * n_col) + j, (i ^ 1) * n_col + (j ^ 1)) for i in range(n_row) for j in range(n_col)]
    chip = squares + lax.ppermute(squares, "row", swap)
    neighbour = lax.ppermute(squares, "col", beside_x) + lax.ppermute(squares, both, across)
    squares = chip + neighbour
    group = [
        [
            (2 * pair + which) * n_col + c
            for pair in range(chips)
            for c in range(n_col)
            if c % 4 in ends
        ]
        for which in range(2)
        for ends in ((0, 3), (1, 2))
    ]
    copies = jnp.broadcast_to(squares[None], (len(group[0]),) + squares.shape)
    squares = lax.all_to_all(copies, both, 0, 0, axis_index_groups=group)
    factor_a, col_scale = finish(squares, solved, rows_i * n_row)
    return (factor_a, col_scale[0])


def solution(mesh):
    return jax.shard_map(
        local,
        mesh=mesh,
        in_specs=(P(None, "row", "col"), P("col", "row"), P()),
        out_specs=(P(both, None), P()),
        check_vma=False,
    )
```
